512 devices in a mesh: dp: 64 (over z, x), tensor: 8 (over y, core).
Axes of the slice: x: 4, y: 4, z: 16, core: 2. Of those that a mesh axis runs over, the one named last changes fastest.
Arguments:
- queries: bfloat16 [16384, 4096], P('dp', 'tensor'), may hold values from -8 to 8
- neighbour_keys: bfloat16 [512, 128, 4096], P('dp', None, 'tensor'), may hold values from -8 to 8
- neighbour_values: bfloat16 [512, 128, 4096], P('dp', None, 'tensor'), may hold values from -6 to 6
- residual: bfloat16 [16384, 4096], P(('dp', 'tensor')), may hold values from -1.5 to 1.5
- out_weight: bfloat16 [4096, 4096], P('tensor', 'dp'), may hold values from -0.09375 to 0.09375
- drop_mask: int32 [16384, 4096], P(('dp', 'tensor')), may hold values 0 or 1
- norm_gain: float32 [4096], replicated, may hold values from 0.5 to 1.5
- norm_bias: float32 [4096], replicated, may hold values from -0.5 to 0.5
- neighbour_owner: int32 [256, 2], P('dp'), may hold values from 0 to 63, as said below
- neighbour_slot: int32 [256, 2], P('dp'), may hold values from 0 to 7, as said below
Outputs:
- residual_next: bfloat16 [16384, 4096], P(('dp', 'tensor'))
- layer_normed: bfloat16 [16384, 4096], P(('dp', 'tensor'))
The draws below stay inside these ranges and needn't reach their ends.
Inputs may be any that keep to these rules, and one draw needn't show every extreme that they name: `neighbour_owner`: the 8 neighbours of the blocks of one dp index are stored on 8 different devices. A device receives at most 12 of all blocks' neighbour requests, and some device exactly that many. `neighbour_slot`: several blocks may use the same stored row.
All inputs are finite; a program needn't handle non-finite values. No bound on the sum of `drop_mask` on one device may be relied on, other than what follows from the above.
Results may differ from the reference program's by a relative error of at most 0.017.
Values may be sent and summed in bfloat16 or wider, within the bound.
A program may use at most 64 MiB of HBM per device.

```python
import jax
import jax.numpy as jnp
from jax import lax

D = 4096
HEADS = 32
HEAD = 128
SPAN = 64
NBR_LEN = 128
NBRS = 2
C_DEV = 4
OWN_CAP = 8
TOKENS = 16384
NCH = 256
NBR_SLOTS = 512
QK_WIDTH = 4096


def owner_layout(key):
    devices = NCH // C_DEV
    per_device = NBRS * C_DEV
    most = min(devices, per_device + per_device // 2)
    pair_count = devices // 2
    paired = jax.random.permutation(jax.random.fold_in(key, 11), devices)
    transfer = jax.random.randint(jax.random.fold_in(key, 12), (pair_count,), 0, most - per_device + 1)
    transfer = transfer.at[0].set(most - per_device)
    counts = jnp.full((devices,), per_device, jnp.int32)
    counts = counts.at[paired[0::2]].add(transfer).at[paired[1::2]].add(-transfer)
    ordering = jax.random.permutation(jax.random.fold_in(key, 13), devices)
    ordered = counts[ordering]
    run_ends = jnp.cumsum(ordered)
    run_starts = run_ends - ordered
    position = jnp.arange(devices * per_device, dtype=jnp.int32)
    run_index = jnp.sum((run_ends[None, :] <= position[:, None]).astype(jnp.int32), axis=1)
    owners = ordering[run_index]
    slots_at = (position - run_starts[run_index]) % OWN_CAP
    owners = owners.reshape(per_device, devices).T.reshape(NCH, NBRS)
    slots_at = slots_at.reshape(per_device, devices).T.reshape(NCH, NBRS)
    return (owners.astype(jnp.int32), slots_at.astype(jnp.int32))


def draw_neighbour_owner(key, part):
    layout = owner_layout(key)
    return layout[0]


def draw_neighbour_slot(key, part):
    layout = owner_layout(key)
    return layout[1]


def draw_queries(key, part):
    key = jax.random.fold_in(key, 4)
    drawn = jnp.clip(1.5 * jax.random.normal(jax.random.fold_in(key, 1), (TOKENS, HEADS * HEAD), jnp.float32), -7.0, 7.0)
    return drawn.astype(jnp.bfloat16)


def draw_neighbour_keys(key, part):
    key = jax.random.fold_in(key, 5)
    drawn = jnp.clip(jax.random.normal(jax.random.fold_in(key, 1), (NBR_SLOTS, NBR_LEN, HEADS * HEAD), jnp.float32), -7.0, 7.0)
    return drawn.astype(jnp.bfloat16)


def set_ends(values, stream_key, smallest, largest):
    spot = [jax.random.randint(jax.random.fold_in(stream_key, axis), (), 0, length) for axis, length in enumerate(values.shape)]
    longest = values.shape.index(max(values.shape))
    beside = spot[:longest] + [(spot[longest] + 1) % values.shape[longest]] + spot[longest + 1:]
    return values.at[tuple(spot)].set(smallest).at[tuple(beside)].set(largest)


def levels(own_key, dims, pieces, smallest, top_value):
    level = 1.0
    for axis_at, shards_of in pieces:
        heights = jax.random.uniform(jax.random.fold_in(jax.random.fold_in(own_key, 6), axis_at), (shards_of,), jnp.float32, smallest / len(pieces), top_value / len(pieces))
        level = level * jnp.repeat(jnp.exp(heights), dims[axis_at] // shards_of).reshape((-1,) + (1,) * (len(dims) - 1 - axis_at))
    return level


def normal_values(stream_key, shape, deviation, limit, cuts=(), kind=jnp.bfloat16):
    gain = levels(stream_key, shape, cuts, -0.22, 0.18) if cuts else 1.0
    result = jax.random.normal(stream_key, shape, jnp.float32) * deviation * gain
    return jnp.minimum(jnp.maximum(result, -limit), limit).astype(kind)


def setup_inputs(seed: int = 0) -> dict:
    splits = jax.random.split(jax.random.key(seed), 11)
    queries = draw_queries(jax.random.fold_in(splits[10], 71), 0)
    neighbour_keys = draw_neighbour_keys(jax.random.fold_in(splits[10], 71), 0)
    neighbour_values = normal_values(splits[2], (NBR_SLOTS, NBR_LEN, QK_WIDTH), 1.0, 6.0, ((0, 64), (2, 8)))
    residual = normal_values(splits[3], (TOKENS, D), 0.25, 1.5, ((0, 512),))
    out_weight = normal_values(splits[4], (QK_WIDTH, D), QK_WIDTH ** -0.5, 0.09375, ((0, 8), (1, 64)))
    drop_mask = set_ends((jax.random.randint(splits[5], (TOKENS, D), 0, 10) < 9).astype(jnp.int32), jax.random.fold_in(splits[5], 1), 0, 1)
    norm_gain = jnp.clip(1.0 + 0.1 * jax.random.normal(splits[6], (D,), jnp.float32), 0.5, 1.5)
    norm_bias = jnp.clip(jax.random.uniform(splits[7], (D,), jnp.float32, -0.5, 0.5), -0.5, 0.5)
    neighbour_owner = draw_neighbour_owner(jax.random.fold_in(splits[10], 71), 0)
    neighbour_slot = draw_neighbour_slot(jax.random.fold_in(splits[10], 71), 0)
    return {"queries": queries, "neighbour_keys": neighbour_keys, "neighbour_values": neighbour_values, "residual": residual, "out_weight": out_weight, "drop_mask": drop_mask, "norm_gain": norm_gain, "norm_bias": norm_bias, "neighbour_owner": neighbour_owner, "neighbour_slot": neighbour_slot}


keep_rate = 0.9
norm_eps = 1e-05

def attend_block(query_rows, key_rows, value_rows):
    count_b, count_r, row_width = query_rows.shape
    length = key_rows.shape[1]
    heads_here = row_width // HEAD
    query_heads = query_rows.reshape(count_b, count_r, heads_here, HEAD).astype(jnp.float32)
    key_heads = key_rows.reshape(count_b, length, heads_here, HEAD).astype(jnp.float32)
    value_heads = value_rows.reshape(count_b, length, heads_here, HEAD).astype(jnp.float32)
    scores = jnp.einsum('brhe,blhe->bhrl', query_heads, key_heads) * HEAD ** (-0.5)
    peak_rows = lax.optimization_barrier(jnp.max(scores, axis=-1))
    raised = jnp.exp(scores - peak_rows[..., None])
    totals = lax.optimization_barrier(jnp.sum(raised, axis=-1))
    weights = (raised / totals[..., None]).astype(jnp.bfloat16).astype(jnp.float32)
    partial_value = jnp.einsum('bhrl,blhe->brhe', weights, value_heads)
    partial_value = partial_value.astype(jnp.bfloat16).reshape(count_b, count_r, row_width)
    return (partial_value, jnp.transpose(peak_rows, (0, 2, 1)), jnp.transpose(totals, (0, 2, 1)))

def merge_pair(partials, peak_rows, totals):
    highest = lax.optimization_barrier(jnp.max(peak_rows, axis=1, keepdims=True))
    merge_weight = totals * jnp.exp(peak_rows - highest)
    weight_sum = lax.optimization_barrier(jnp.sum(merge_weight, axis=1))
    part_shape = partials.shape
    part_heads = partials.reshape(part_shape[0], part_shape[1], part_shape[2], -1, HEAD).astype(jnp.float32)
    combined = lax.optimization_barrier(jnp.sum(part_heads * merge_weight[..., None], axis=1)) / weight_sum[..., None]
    return combined.reshape(part_shape[0], part_shape[2], part_shape[3]).astype(jnp.bfloat16)

def reference(queries, neighbour_keys, neighbour_values, residual, out_weight, drop_mask, norm_gain, norm_bias, neighbour_owner, neighbour_slot):
    row_width = HEADS * HEAD
    shifted = jnp.concatenate([jnp.zeros((1, row_width), queries.dtype), queries[:-1]], axis=0)
    shifted = shifted.reshape(NCH, SPAN, row_width)
    store_index = (neighbour_owner * OWN_CAP + neighbour_slot).astype(jnp.int32)

    def one_block(block_items):
        block_rows, block_index = block_items
        gathered_keys = jnp.take(neighbour_keys, block_index, axis=0)
        gathered_values = jnp.take(neighbour_values, block_index, axis=0)
        repeated = jnp.broadcast_to(block_rows[None], (NBRS, SPAN, row_width))
        partial_value, peak_rows, totals = attend_block(repeated, gathered_keys, gathered_values)
        return merge_pair(partial_value[None], peak_rows[None], totals[None])[0]
    merged = lax.map(one_block, (shifted, store_index))
    flat_rows = merged.reshape(TOKENS, row_width)
    cross_rows = jnp.concatenate([flat_rows[1:], jnp.zeros((1, row_width), flat_rows.dtype)], axis=0)
    branch = jnp.dot(cross_rows, out_weight, preferred_element_type=jnp.float32)
    keep_scale = drop_mask.astype(jnp.float32) * (1.0 / keep_rate)
    stream = residual.astype(jnp.float32) + keep_scale * branch
    centre = lax.optimization_barrier(jnp.mean(stream, axis=1, keepdims=True))
    spread = lax.optimization_barrier(jnp.mean(jnp.square(stream - centre), axis=1, keepdims=True))
    normed = (stream - centre) * lax.rsqrt(spread + norm_eps) * norm_gain + norm_bias
    return (stream.astype(jnp.bfloat16), normed.astype(jnp.bfloat16))
```

```python
import functools

import jax
import jax.numpy as jnp
from jax import lax
from jax.experimental import pallas as pl
from jax.experimental.pallas import tpu as pltpu
from jax.sharding import PartitionSpec as P

HEAD = 128
XN = 4
CAP = 12
HALF = CAP // 2
SROWS = 16
GROUP = 2
NONE = -1e30

keep_rate = 0.9
norm_eps = 1e-05
MESH = pl.DeviceIdType.MESH


def shifted(x, axis, by):
    count = lax.axis_size(axis)
    pairs = [(i, i + by) for i in range(count) if 0 <= i + by < count]
    return lax.ppermute(x, axis, pairs)


def routing_tables(owner, slot, capacity):
    blocks, nbrs = owner.shape
    per = blocks * nbrs
    me = lax.axis_index("dp")
    z, x = me // XN, me % XN
    code = (owner * capacity + slot).reshape(per)
    every = lax.all_gather(code, "dp", axis=0, tiled=True)
    count = every.shape[0]
    zn = count // per // XN
    own = every // capacity
    row = every % capacity
    i = jnp.arange(count, dtype=jnp.int32)
    src = i // per
    z0, x0 = src // XN, src % XN
    block = z0 * blocks + (i // nbrs) % blocks
    rank = jnp.sum(
        ((own[None, :] == own[:, None]) & (i[None, :] < i[:, None])).astype(jnp.int32), axis=1
    )
    j = jnp.arange(CAP, dtype=jnp.int32)
    rel = jnp.arange(XN, dtype=jnp.int32)
    target = z * XN + (x + rel) % XN
    hit = (
        (own[None, None, :] == target[:, None, None])
        & (rank[None, None, :] == j[None, :, None])
        & (x0[None, None, :] == x)
    )
    pick = jnp.max(jnp.where(hit, block[None, None, :], -1), axis=-1)
    mine = (own[None, :] == me) & (rank[None, :] == j[:, None])
    store = jnp.max(jnp.where(mine, row[None, :], 0), axis=-1)
    back = (x0[None, :] - x + XN) % XN
    way = jnp.where(
        back == 0,
        0,
        jnp.where(
            back == 3,
            1,
            jnp.where(back == 1, 2, jnp.where(j[:, None] < HALF, 1, 2)),
        ),
    )
    path = jnp.max(jnp.where(mine, way, 0), axis=-1)
    col_own = lax.dynamic_index_in_dim(own.reshape(zn, XN, per), x, 1, keepdims=False)
    col_rank = lax.dynamic_index_in_dim(rank.reshape(zn, XN, per), x, 1, keepdims=False)
    here = (col_own // XN) == z
    place = (col_own % XN - x + XN) % XN
    data_at = jnp.where(here, place * CAP + col_rank, 0)
    stat_at = jnp.where(here, place * SROWS + col_rank, CAP)
    return jnp.concatenate(
        [pick.reshape(-1), store, path, data_at.reshape(-1), stat_at.reshape(-1)]
    ).astype(jnp.int32)


def route_kernel(zn, blocks, tab, q_ref, k_ref, v_ref, out_ref, *scratch):
    groups = q_ref.shape[0]
    span = q_ref.shape[2]
    wide = q_ref.shape[3]
    me = lax.axis_index("dp")
    tens = lax.axis_index("tensor")
    z, x = me // XN, me % XN
    z_up = ((z + 1) % zn) * XN + x
    z_dn = ((z + zn - 1) % zn) * XN + x
    x_up = z * XN + (x + 1) % XN
    x_dn = z * XN + (x + XN - 1) % XN
    per_g = 11
    bufs = [scratch[g * per_g : (g + 1) * per_g] for g in range(groups)]
    (
        lse_acc,
        w_scr,
        ag_send,
        ag_recv,
        x_send,
        x_recv,
        rd_send,
        rd_recv,
        rs_send,
        rs_recv,
    ) = scratch[groups * per_g :]
    PICK, STORE, PATH = 0, XN * CAP, XN * CAP + CAP
    DATA = XN * CAP + 2 * CAP
    STAT = DATA + zn * blocks * 2
    hb = blocks // 2
    chains = [(1, 0, zn // 2), (1, 1, zn // 2 - 1), (-1, 0, zn // 2 - 1), (-1, 1, zn // 2)]
    started = []

    barrier = pltpu.get_barrier_semaphore()
    for peer in (z_up, z_dn, x_up, x_dn):
        pl.semaphore_signal(barrier, inc=1, device_id=(peer, tens), device_id_type=MESH)
    pl.semaphore_wait(barrier, 4)

    def remote(src, dst, send, recv, peer):
        copy = pltpu.make_async_remote_copy(
            src_ref=src,
            dst_ref=dst,
            send_sem=send,
            recv_sem=recv,
            device_id=(peer, tens),
            device_id_type=MESH,
        )
        copy.start()
        started.append(copy)
        return copy

    def gather(g):
        col = bufs[g][0]
        for b in range(blocks):
            col[z * blocks + b] = q_ref[g, b]
        for s in range(zn // 2 + 1):
            for c, (way, half, steps) in enumerate(chains):
                if s > steps:
                    continue
                at = ((z - way * s + zn) % zn) * blocks + half * hb
                here = col.at[pl.ds(at, hb)]
                if s > 0:
                    pltpu.make_async_remote_copy(
                        src_ref=here,
                        dst_ref=here,
                        send_sem=ag_send.at[g, c, s - 1],
                        recv_sem=ag_recv.at[g, c, s - 1],
                        device_id=(z_up, tens),
                        device_id_type=MESH,
                    ).wait_recv()
                if s < steps:
                    src = q_ref.at[g, pl.ds(half * hb, hb)] if s == 0 else here
                    remote(
                        src,
                        here,
                        ag_send.at[g, c, s],
                        ag_recv.at[g, c, s],
                        z_up if way > 0 else z_dn,
                    )
            yield

    def exchange(g):
        col, s1r, s1l, a1l, a1r, s2, a2, res, stat, _, _ = bufs[g]

        def pick(rel, j):
            return col[jnp.maximum(tab[PICK + rel * CAP + j], 0)]

        def asked(rel, j):
            return tab[PICK + rel * CAP + j] >= 0

        @pl.loop(0, HALF)
        def _(j):
            s1r[j] = pick(2, j)
            s1l[j] = pick(2, j + HALF)

        step1r = remote(s1r, a1l, x_send.at[g, 0], x_recv.at[g, 0], x_up)
        step1l = remote(s1l, a1r, x_send.at[g, 1], x_recv.at[g, 1], x_dn)

        @pl.loop(0, HALF)
        def _(j):
            s2[0, j + HALF] = pick(1, j + HALF)
            s2[1, j] = pick(3, j)

        lo, hi = pl.ds(0, HALF), pl.ds(HALF, HALF)
        step2 = [
            remote(s2.at[0, hi], a2.at[0, hi], x_send.at[g, 2], x_recv.at[g, 2], x_up),
            remote(s2.at[1, lo], a2.at[1, lo], x_send.at[g, 3], x_recv.at[g, 3], x_dn),
        ]
        yield
        step1r.wait_recv()
        step1l.wait_recv()

        @pl.loop(0, HALF)
        def _(j):
            s2[0, j] = jnp.where(asked(1, j), pick(1, j), a1l[j])
            s2[1, j + HALF] = jnp.where(asked(3, j + HALF), pick(3, j + HALF), a1r[j])

        step2 += [
            remote(s2.at[0, lo], a2.at[0, lo], x_send.at[g, 4], x_recv.at[g, 4], x_up),
            remote(s2.at[1, hi], a2.at[1, hi], x_send.at[g, 5], x_recv.at[g, 5], x_dn),
        ]
        yield
        for copy in step2:
            copy.wait_recv()

        lane = lax.broadcasted_iota(jnp.int32, (span, HEAD), 1)

        @pl.loop(0, CAP)
        def _(j):
            path = tab[PATH + j]
            rows = jnp.where(
                path == 0, pick(0, j), jnp.where(path == 1, a2[0, j], a2[1, j])
            )
            at = tab[STORE + j]
            for h in range(GROUP):
                here = slice(h * HEAD, (h + 1) * HEAD)
                cols = slice((g * GROUP + h) * HEAD, (g * GROUP + h + 1) * HEAD)
                scores = lax.dot_general(
                    rows[:, here],
                    k_ref[at, :, cols],
                    (((1,), (1,)), ((), ())),
                    preferred_element_type=jnp.float32,
                ) * HEAD ** (-0.5)
                peak = jnp.max(scores, axis=-1, keepdims=True)
                raised = jnp.exp(scores - peak)
                total = jnp.sum(raised, axis=-1, keepdims=True)
                prob = (raised / total).astype(jnp.bfloat16)
                part = jnp.dot(prob, v_ref[at, :, cols], preferred_element_type=jnp.float32)
                res[j, :, here] = part.astype(jnp.bfloat16)
                old = lse_acc[h * span : (h + 1) * span, :]
                lse_acc[h * span : (h + 1) * span, :] = jnp.where(
                    lane == j, peak + jnp.log(total), old
                )

        turned = jnp.transpose(lse_acc[...])[0:SROWS]
        slot_row = lax.broadcasted_iota(jnp.int32, turned.shape, 0)
        stat[0:SROWS, :] = jnp.where(slot_row < CAP, turned, NONE)

        def part_of(rel, first):
            return res.at[pl.ds(rel * CAP + first, HALF)]

        def stats_of(rel, first=0, rows=SROWS):
            return stat.at[pl.ds(rel * SROWS + first, rows)]

        def send(src, dst, at, peer):
            return remote(src, dst, x_send.at[g, at], x_recv.at[g, at], peer)

        r_lo = send(part_of(0, 0), part_of(3, 0), 6, x_up)
        l_hi = send(part_of(0, HALF), part_of(1, HALF), 7, x_dn)
        r_st = send(stats_of(0), stats_of(3), 8, x_up)
        l_st = send(stats_of(0), stats_of(1), 9, x_dn)
        r_hi = send(part_of(0, HALF), part_of(3, HALF), 10, x_up)
        l_lo = send(part_of(0, 0), part_of(1, 0), 11, x_dn)
        yield
        r_lo.wait_recv()
        f_r = send(part_of(3, 0), part_of(2, 0), 12, x_up)
        l_hi.wait_recv()
        f_l = send(part_of(1, HALF), part_of(2, HALF), 13, x_dn)
        r_st.wait_recv()
        f_rs = send(stats_of(3, 0, 8), stats_of(2, 0, 8), 14, x_up)
        l_st.wait_recv()
        f_ls = send(stats_of(1, 8, 8), stats_of(2, 8, 8), 15, x_dn)
        yield
        for copy in (r_hi, l_lo, f_r, f_l, f_rs, f_ls):
            copy.wait_recv()
        yield

    def combine(g, z0, half, arrived, dst, dst_stat, scr):
        res, stat = bufs[g][7], bufs[g][8]
        count = len(arrived) + 2
        for b in range(hb):
            base = (z0 * blocks + half * hb + b) * 2
            lses = [ref[b : b + 1, :] for _, ref in arrived]
            lses += [stat[pl.ds(tab[STAT + base + r], 1), :] for r in range(2)]
            top = functools.reduce(jnp.maximum, lses)
            weights = [jnp.exp(v - top) for v in lses]
            total = functools.reduce(jnp.add, weights)
            for n, w in enumerate(weights):
                w_scr[scr, b, n : n + 1, :] = w / total
            if dst_stat is not None:
                dst_stat[b : b + 1, :] = top + jnp.log(total)
        for b in range(hb):
            base = (z0 * blocks + half * hb + b) * 2
            cols = jnp.transpose(w_scr[scr, b])
            vals = [ref[b] for ref, _ in arrived]
            vals += [res[tab[DATA + base + r]] for r in range(2)]
            outs = []
            for h in range(GROUP):
                here = slice(h * HEAD, (h + 1) * HEAD)
                w = cols[h * span : (h + 1) * span]
                acc = vals[0][:, here].astype(jnp.float32) * w[:, 0:1]
                for n in range(1, count):
                    acc += vals[n][:, here].astype(jnp.float32) * w[:, n : n + 1]
                outs.append(acc.astype(jnp.bfloat16))
            dst[b] = jnp.concatenate(outs, axis=1)

    def reduce(g):
        ring, ring_stat = bufs[g][9], bufs[g][10]
        for s in range(zn // 2 + 1):
            for c, (way, half, steps) in enumerate(chains):
                i = s - (zn // 2 - steps)
                if i < 0 or i > steps:
                    continue
                here, here_stat = ring.at[c, i], ring_stat.at[c, i]
                peer = z_up if way > 0 else z_dn
                if i > 0:
                    for ref, snd, rcv in (
                        (here, rd_send, rd_recv),
                        (here_stat, rs_send, rs_recv),
                    ):
                        pltpu.make_async_remote_copy(
                            src_ref=ref,
                            dst_ref=ref,
                            send_sem=snd.at[g, c, i - 1],
                            recv_sem=rcv.at[g, c, i - 1],
                            device_id=(peer, tens),
                            device_id_type=MESH,
                        ).wait_recv()
                if i < steps:
                    z0 = (z + way * (steps - i) + zn) % zn
                    arrived = [(here, here_stat)] if i > 0 else []
                    combine(g, z0, half, arrived, here, here_stat, c)
                    remote(
                        here,
                        ring.at[c, i + 1],
                        rd_send.at[g, c, i],
                        rd_recv.at[g, c, i],
                        peer,
                    )
                    remote(
                        here_stat,
                        ring_stat.at[c, i + 1],
                        rs_send.at[g, c, i],
                        rs_recv.at[g, c, i],
                        peer,
                    )
            yield
        for half in range(2):
            arrived = [
                (ring.at[c, steps], ring_stat.at[c, steps])
                for c, (_, part, steps) in enumerate(chains)
                if part == half
            ]
            combine(
                g, z, half, arrived, out_ref.at[g, pl.ds(half * hb, hb)], None, half
            )
        yield

    def weave(first, second):
        live = [iter(first), iter(second)]
        while live:
            live = [it for it in live if next(it, "end") != "end"]

    def run(it):
        for _ in it:
            pass

    run(gather(0))
    for g in range(1, groups):
        weave(gather(g), exchange(g - 1)) if g == 1 else weave(reduce(g - 2), gather(g))
    weave(reduce(groups - 2), exchange(groups - 1))
    run(reduce(groups - 1))
    for copy in started:
        copy.wait_send()


def route(tab, q, k, v):
    groups, blocks, span, wide = q.shape
    zn = lax.axis_size("dp") // XN
    steps = zn // 2
    bf, f32 = jnp.bfloat16, jnp.float32
    per_group = [
        pltpu.VMEM((zn * blocks, span, wide), bf),
        pltpu.VMEM((HALF, span, wide), bf),
        pltpu.VMEM((HALF, span, wide), bf),
        pltpu.VMEM((HALF, span, wide), bf),
        pltpu.VMEM((HALF, span, wide), bf),
        pltpu.VMEM((2, CAP, span, wide), bf),
        pltpu.VMEM((2, CAP, span, wide), bf),
        pltpu.VMEM((XN * CAP, span, wide), bf),
        pltpu.VMEM((XN * SROWS, HEAD), f32),
        pltpu.VMEM((4, steps + 1, blocks // 2, span, wide), bf),
        pltpu.VMEM((4, steps + 1, 8, HEAD), f32),
    ]
    dma = pltpu.SemaphoreType.DMA
    vmem = pl.BlockSpec(memory_space=pltpu.VMEM)
    return pl.pallas_call(
        functools.partial(route_kernel, zn, blocks),
        out_shape=jax.ShapeDtypeStruct(q.shape, bf),
        in_specs=[pl.BlockSpec(memory_space=pltpu.SMEM), vmem, vmem, vmem],
        out_specs=vmem,
        scratch_shapes=per_group * groups
        + [
            pltpu.VMEM((GROUP * span, HEAD), f32),
            pltpu.VMEM((4, 2, 8, HEAD), f32),
            dma((groups, 4, steps)),
            dma((groups, 4, steps)),
            dma((groups, 16)),
            dma((groups, 16)),
            dma((groups, 4, steps)),
            dma((groups, 4, steps)),
            dma((groups, 4, steps)),
            dma((groups, 4, steps)),
        ],
        compiler_params=pltpu.CompilerParams(
            collective_id=0, has_side_effects=True, vmem_limit_bytes=48 * 1024 * 1024
        ),
        cost_estimate=pl.CostEstimate(
            flops=400_000_000, bytes_accessed=16_000_000, transcendentals=400_000
        ),
    )(tab, q, k, v)


def local(
    queries,
    neighbour_keys,
    neighbour_values,
    residual,
    out_weight,
    drop_mask,
    norm_gain,
    norm_bias,
    neighbour_owner,
    neighbour_slot,
):
    row_width = queries.shape[1]
    blocks = neighbour_owner.shape[0]
    span = queries.shape[0] // blocks
    wide = GROUP * HEAD
    groups = row_width // wide
    tab = routing_tables(neighbour_owner, neighbour_slot, neighbour_keys.shape[0])
    carried = shifted(queries[-1:], "dp", 1)
    asked = jnp.concatenate([carried, queries[:-1]], axis=0)
    asked = asked.reshape(blocks, span, groups, wide).transpose(2, 0, 1, 3)
    merged = route(tab, asked, neighbour_keys, neighbour_values)
    flat_rows = merged.transpose(1, 2, 0, 3).reshape(-1, row_width)
    following = shifted(flat_rows[:1], "dp", -1)
    cross_rows = jnp.concatenate([flat_rows[1:], following], axis=0)
    whole_weight = lax.all_gather(out_weight, "dp", axis=1, tiled=True)
    branch = lax.psum_scatter(
        jnp.dot(cross_rows, whole_weight, preferred_element_type=jnp.float32).astype(jnp.bfloat16),
        "tensor",
        scatter_dimension=0,
        tiled=True,
    ).astype(jnp.float32)
    keep_scale = drop_mask.astype(jnp.float32) * (1.0 / keep_rate)
    stream = residual.astype(jnp.float32) + keep_scale * branch
    centre = jnp.mean(stream, axis=1, keepdims=True)
    spread = jnp.mean(jnp.square(stream - centre), axis=1, keepdims=True)
    normed = (stream - centre) * lax.rsqrt(spread + norm_eps) * norm_gain + norm_bias
    return (stream.astype(jnp.bfloat16), normed.astype(jnp.bfloat16))


def solution(mesh):
    placed = (
        P("dp", "tensor"),
        P("dp", None, "tensor"),
        P("dp", None, "tensor"),
        P(("dp", "tensor"), None),
        P("tensor", "dp"),
        P(("dp", "tensor"), None),
        P(),
        P(),
        P("dp", None),
        P("dp", None),
    )
    return jax.shard_map(
        local,
        mesh=mesh,
        in_specs=placed,
        out_specs=(P(("dp", "tensor"), None), P(("dp", "tensor"), None)),
        check_vma=False,
    )
```

```python
import functools

import jax
import jax.numpy as jnp
from jax import lax
from jax.experimental import pallas as pl
from jax.experimental.pallas import tpu as pltpu
from jax.sharding import PartitionSpec as P

HEAD = 128
XN = 4
GROUP = 2
NONE = -1e30

keep_rate = 0.9
norm_eps = 1e-05
MESH = pl.DeviceIdType.MESH


ORDER = (
    "k0 c g0 g1",
    "c g0 g1",
    "c g0 g1",
    "c g0 g1",
    "c g0 g1 k0 k1",
    "c g0 g1",
    "c g0 g1",
    "c g0 g1",
    "c*2 g0 g1",
    "k0 r0",
    "r0",
    "r0 k1",
    "r0",
    "k1 r0 r1",
) + ("r0 r1",) * 5 + ("r1*6",)


def shifted(x, axis, by):
    count = lax.axis_size(axis)
    pairs = [(i, i + by) for i in range(count) if 0 <= i + by < count]
    return lax.ppermute(x, axis, pairs)


def route_kernel(zn, blocks, code_ref, q_ref, k_ref, v_ref, out_ref, *scratch):
    groups = q_ref.shape[0]
    span = q_ref.shape[3] // GROUP
    wide = GROUP * HEAD
    rows = k_ref.shape[0]
    me = lax.axis_index("dp")
    tens = lax.axis_index("tensor")
    z, x = me // XN, me % XN
    z_up = ((z + 1) % zn) * XN + x
    z_dn = ((z + zn - 1) % zn) * XN + x
    x_up = z * XN + (x + 1) % XN
    x_dn = z * XN + (x + XN - 1) % XN
    per_g = 7
    bufs = [scratch[g * per_g : (g + 1) * per_g] for g in range(groups)]
    (
        codes,
        table,
        slots,
        code_send,
        code_recv,
        ag_send,
        ag_recv,
        kv_own,
        kv_send,
        kv_recv,
        rd_send,
        rd_recv,
        rs_send,
        rs_recv,
        table_sem,
    ) = scratch[groups * per_g :]
    far, near = zn // 2, zn // 2 - 1
    chains = [
        (way, b, far if (b < blocks // 2) == (way > 0) else near)
        for b in range(blocks)
        for way in (1, -1)
    ]
    started = []

    barrier = pltpu.get_barrier_semaphore()
    for peer in (z_up, z_dn, x_up, x_dn):
        pl.semaphore_signal(barrier, inc=1, device_id=(peer, tens), device_id_type=MESH)
    pl.semaphore_wait(barrier, 4)

    def copy_to(src, dst, send, recv, peer):
        return pltpu.make_async_remote_copy(
            src_ref=src,
            dst_ref=dst,
            send_sem=send,
            recv_sem=recv,
            device_id=(peer, tens),
            device_id_type=MESH,
        )

    def remote(src, dst, send, recv, peer):
        copy = copy_to(src, dst, send, recv, peer)
        copy.start()
        started.append(copy)
        return copy

    def stores(g):
        hb = rows // 2
        lo, hi = pl.ds(0, hb), pl.ds(hb, hb)
        cols = pl.ds(g * wide, wide)
        pairs = [(k_ref, bufs[g][1]), (v_ref, bufs[g][2])]
        own, first, later = [], [], []
        for n, (src, dst) in enumerate(pairs):
            whole = src.at[:, :, cols] if n == 0 else src.at[:, g]
            copy = pltpu.make_async_copy(whole, dst.at[0], kv_own.at[g, n])
            copy.start()
            own.append(copy)
        for part, place, peer, at in ((lo, 3, x_up, 0), (hi, 1, x_dn, 1), (hi, 3, x_up, 2), (lo, 1, x_dn, 3)):
            for n, (src, dst) in enumerate(pairs):
                copy = remote(
                    src.at[part, :, cols] if n == 0 else src.at[part, g],
                    dst.at[place, part],
                    kv_send.at[g, n, at],
                    kv_recv.at[g, n, at],
                    peer,
                )
                (first if at < 2 else later).append(copy)
        yield
        for i, (part, place, peer, at) in enumerate(((lo, 3, x_up, 4), (hi, 1, x_dn, 5))):
            for n, (_, dst) in enumerate(pairs):
                first[2 * i + n].wait_recv()
                later.append(
                    remote(
                        dst.at[place, part],
                        dst.at[2, part],
                        kv_send.at[g, n, at],
                        kv_recv.at[g, n, at],
                        peer,
                    )
                )
        yield
        for copy in own:
            copy.wait()
        for copy in later:
            copy.wait_recv()
        yield

    def gather_codes():
        codes[z] = code_ref[...]
        for s in range(far + 1):
            for c, (way, steps) in enumerate(((1, far), (-1, near))):
                if s > steps:
                    continue
                here = codes.at[(z - way * s + zn) % zn]
                peer = z_up if way > 0 else z_dn
                if s > 0:
                    copy_to(here, here, code_send.at[c, s - 1], code_recv.at[c, s - 1], peer).wait_recv()
                if s < steps:
                    src = code_ref if s == 0 else here
                    remote(src, here, code_send.at[c, s], code_recv.at[c, s], peer)
            yield
        copy = pltpu.make_async_copy(codes, table, table_sem)
        copy.start()
        copy.wait()

        @pl.loop(0, zn)
        def _(z0):
            asks = [table[z0, 0, k] for k in range(2 * blocks)]
            for r in range(XN):
                first = (z * XN + (x + r) % XN) * rows
                block, at = jnp.int32(0), jnp.int32(0)
                for k, ask in enumerate(asks):
                    hit = (ask >= first) & (ask < first + rows)
                    block = jnp.where(hit, k // 2, block)
                    at = jnp.where(hit, ask - first, at)
                slots[z0, r] = z0 * blocks + block
                slots[z0, XN + r] = at
            for k, ask in enumerate(asks):
                holder = ask // rows
                there = holder // XN == z
                slots[z0, 2 * XN + k] = jnp.where(there, (holder - x + XN) % XN, XN)

        yield

    def gather(g):
        col = bufs[g][0]
        for b in range(blocks):
            col[z * blocks + b] = q_ref[g, b]
        for s in range(far + 1):
            for c, (way, block, steps) in enumerate(chains):
                if s > steps:
                    continue
                here = col.at[((z - way * s + zn) % zn) * blocks + block]
                peer = z_up if way > 0 else z_dn
                if s > 0:
                    copy_to(
                        here, here, ag_send.at[g, c, s - 1], ag_recv.at[g, c, s - 1], peer
                    ).wait_recv()
                if s < steps:
                    src = q_ref.at[g, block] if s == 0 else here
                    remote(src, here, ag_send.at[g, c, s], ag_recv.at[g, c, s], peer)
            yield

    left = lax.broadcasted_iota(jnp.int32, (HEAD, GROUP * span), 1) < span
    left_bf = left.astype(jnp.float32).astype(jnp.bfloat16)
    right_bf = (1.0 - left.astype(jnp.float32)).astype(jnp.bfloat16)

    def attend(g, z0):
        col, keys, values, res, stat = bufs[g][:5]
        scale = HEAD ** (-0.5)
        for pair in range(0, XN, 2):
            places = (pair, pair + 1)
            at = [slots[z0, XN + r] for r in places]
            scores = []
            for r, a in zip(places, at):
                q = col[slots[z0, r]]
                q2 = jnp.concatenate([q * left_bf, q * right_bf], axis=0)
                scores.append(jnp.dot(keys[r, a], q2, preferred_element_type=jnp.float32))
            tops = [jnp.max(v, axis=0, keepdims=True) for v in scores]
            raised = [jnp.exp((v - t) * scale) for v, t in zip(scores, tops)]
            totals = [jnp.sum(v, axis=0, keepdims=True) for v in raised]
            for r, a, e, top, total in zip(places, at, raised, tops, totals):
                eb = e.astype(jnp.bfloat16)
                p2 = jnp.concatenate([eb * left_bf, eb * right_bf], axis=0)
                part = jnp.dot(values[r, a], p2, preferred_element_type=jnp.float32)
                res[z0 * XN + r] = (part * (1.0 / total)).astype(jnp.bfloat16)
                stat[z0, r : r + 1, :] = top * scale + jnp.log(total)
        stat[z0, XN : XN + 1, :] = jnp.full((1, GROUP * span), NONE, jnp.float32)

    def combine(g, z0, block, arrived, dst, dst_stat):
        res, stat = bufs[g][3:5]
        lses = [ref[...] for _, ref in arrived]
        vals = [ref[...] for ref, _ in arrived]
        for r in range(2):
            place = slots[z0, 2 * XN + 2 * block + r]
            lses.append(stat[z0, pl.ds(place, 1), :])
            vals.append(res[z0 * XN + jnp.minimum(place, XN - 1)])
        top = functools.reduce(jnp.maximum, lses)
        weights = [jnp.exp(v - top) for v in lses]
        total = functools.reduce(jnp.add, weights)
        if dst_stat is not None:
            dst_stat[...] = top + jnp.log(total)
        share = 1.0 / total
        acc = vals[0].astype(jnp.float32) * (weights[0] * share)
        for v, w in zip(vals[1:], weights[1:]):
            acc += v.astype(jnp.float32) * (w * share)
        dst[...] = acc.astype(jnp.bfloat16)

    def reduce(g):
        ring, ring_stat = bufs[g][5:7]
        attend(g, (z + far) % zn)
        for s in range(far + 1):
            for c, (way, block, steps) in enumerate(chains):
                i = s - (far - steps)
                if i < 0 or i > steps:
                    continue
                here, here_stat = ring.at[c, i], ring_stat.at[c, i, pl.ds(0, 1)]
                peer = z_up if way > 0 else z_dn
                if i > 0:
                    for ref, snd, rcv in (
                        (here, rd_send, rd_recv),
                        (here_stat, rs_send, rs_recv),
                    ):
                        copy_to(
                            ref, ref, snd.at[g, c, i - 1], rcv.at[g, c, i - 1], peer
                        ).wait_recv()
                if i < steps:
                    z0 = (z + way * (steps - i) + zn) % zn
                    arrived = [(here, here_stat)] if i > 0 else []
                    combine(g, z0, block, arrived, here, here_stat)
                    remote(
                        here_stat,
                        ring_stat.at[c, i + 1, pl.ds(0, 1)],
                        rs_send.at[g, c, i],
                        rs_recv.at[g, c, i],
                        peer,
                    )
                    remote(
                        here,
                        ring.at[c, i + 1],
                        rd_send.at[g, c, i],
                        rd_recv.at[g, c, i],
                        peer,
                    )
            away = far - (s + 1)
            if away > 0:

                @pl.loop(0, 2)
                def _(n):
                    attend(g, (z + (1 - 2 * n) * away + zn) % zn)

            elif away == 0:
                attend(g, z)
            yield
        for b in range(blocks):
            arrived = [
                (ring.at[c, steps], ring_stat.at[c, steps, pl.ds(0, 1)])
                for c, (_, block, steps) in enumerate(chains)
                if block == b
            ]
            combine(g, z, b, arrived, out_ref.at[g, b], None)
        yield

    live = {"c": gather_codes()}
    parts = {"g": gather, "k": stores, "r": reduce}
    for step in ORDER:
        for token in step.split():
            name, times = token.split("*") if "*" in token else (token, "1")
            if name not in live:
                live[name] = parts[name[0]](int(name[1:]))
            for _ in range(int(times)):
                next(live[name], None)
    for it in live.values():
        for _ in it:
            pass
    for copy in started:
        copy.wait_send()


def route(code, q, k, v):
    groups, blocks, deep, wide = q.shape
    rows = k.shape[0]
    zn = lax.axis_size("dp") // XN
    steps = zn // 2
    bf, f32 = jnp.bfloat16, jnp.float32
    per_group = [
        pltpu.VMEM((zn * blocks, deep, wide), bf),
        pltpu.VMEM((XN, rows, k.shape[1], GROUP * HEAD), bf),
        pltpu.VMEM((XN, rows) + v.shape[2:], bf),
        pltpu.VMEM((zn * XN, deep, wide), bf),
        pltpu.VMEM((zn, 8, wide), f32),
        pltpu.VMEM((2 * blocks, steps + 1, deep, wide), bf),
        pltpu.VMEM((2 * blocks, steps + 1, 8, wide), f32),
    ]
    dma = pltpu.SemaphoreType.DMA
    vmem = pl.BlockSpec(memory_space=pltpu.VMEM)
    hbm = pl.BlockSpec(memory_space=pl.ANY)
    ring = dma((groups, 2 * blocks, steps))
    return pl.pallas_call(
        functools.partial(route_kernel, zn, blocks),
        out_shape=jax.ShapeDtypeStruct(q.shape, bf),
        in_specs=[vmem, vmem, hbm, hbm],
        out_specs=vmem,
        scratch_shapes=per_group * groups
        + [
            pltpu.VMEM((zn, 8, HEAD), jnp.int32),
            pltpu.SMEM((zn, 8, HEAD), jnp.int32),
            pltpu.SMEM((zn, 2 * XN + 2 * blocks), jnp.int32),
            dma((2, steps)),
            dma((2, steps)),
            ring,
            ring,
            dma((groups, 2)),
            dma((groups, 2, 6)),
            dma((groups, 2, 6)),
            ring,
            ring,
            ring,
            ring,
            dma,
        ],
        compiler_params=pltpu.CompilerParams(
            collective_id=0, has_side_effects=True, vmem_limit_bytes=56 * 1024 * 1024
        ),
        cost_estimate=pl.CostEstimate(
            flops=1_100_000_000, bytes_accessed=16_000_000, transcendentals=2_200_000
        ),
    )(code, q, k, v)


def local(
    queries,
    neighbour_keys,
    neighbour_values,
    residual,
    out_weight,
    drop_mask,
    norm_gain,
    norm_bias,
    neighbour_owner,
    neighbour_slot,
):
    row_width = queries.shape[1]
    blocks = neighbour_owner.shape[0]
    span = queries.shape[0] // blocks
    groups = row_width // (GROUP * HEAD)
    code = (neighbour_owner * neighbour_keys.shape[0] + neighbour_slot).reshape(1, -1)
    code = jnp.pad(code, ((0, 7), (0, HEAD - code.shape[1])))
    carried = shifted(queries[-1:], "dp", 1)
    asked = jnp.concatenate([carried, queries[:-1]], axis=0)
    asked = asked.reshape(blocks, span, groups, GROUP, HEAD).transpose(2, 0, 4, 3, 1)
    asked = asked.reshape(groups, blocks, HEAD, GROUP * span)
    rows, length, _ = neighbour_values.shape
    values = neighbour_values.reshape(rows, length, groups, GROUP, HEAD).transpose(0, 2, 4, 3, 1)
    values = values.reshape(rows, groups, HEAD, GROUP * length)
    merged = route(code, asked, neighbour_keys, values)
    merged = merged.reshape(groups, blocks, HEAD, GROUP, span).transpose(1, 4, 0, 3, 2)
    flat_rows = merged.reshape(-1, row_width)
    following = shifted(flat_rows[:1], "dp", -1)
    cross_rows = jnp.concatenate([flat_rows[1:], following], axis=0)
    whole_weight = lax.all_gather(out_weight, "dp", axis=1, tiled=True)
    branch = lax.psum_scatter(
        jnp.dot(cross_rows, whole_weight, preferred_element_type=jnp.float32).astype(jnp.bfloat16),
        "tensor",
        scatter_dimension=0,
        tiled=True,
    ).astype(jnp.float32)
    keep_scale = drop_mask.astype(jnp.float32) * (1.0 / keep_rate)
    stream = residual.astype(jnp.float32) + keep_scale * branch
    centre = jnp.mean(stream, axis=1, keepdims=True)
    spread = jnp.mean(jnp.square(stream - centre), axis=1, keepdims=True)
    normed = (stream - centre) * lax.rsqrt(spread + norm_eps) * norm_gain + norm_bias
    return (stream.astype(jnp.bfloat16), normed.astype(jnp.bfloat16))


def solution(mesh):
    placed = (
        P("dp", "tensor"),
        P("dp", None, "tensor"),
        P("dp", None, "tensor"),
        P(("dp", "tensor"), None),
        P("tensor", "dp"),
        P(("dp", "tensor"), None),
        P(),
        P(),
        P("dp", None),
        P("dp", None),
    )
    return jax.shard_map(
        local,
        mesh=mesh,
        in_specs=placed,
        out_specs=(P(("dp", "tensor"), None), P(("dp", "tensor"), None)),
        check_vma=False,
    )
```

```python
import functools

import jax
import jax.numpy as jnp
from jax import lax
from jax.experimental import pallas as pl
from jax.experimental.pallas import tpu as pltpu
from jax.sharding import PartitionSpec as P

HEAD = 128
XN = 4
GROUP = 2
NONE = -1e30

keep_rate = 0.9
norm_eps = 1e-05
MESH = pl.DeviceIdType.MESH


ORDER = (
    [("k0", "c", "g0", "g1")]
    + [("c", "g0", "g1")] * 3
    + [("c", "g0", "g1", "k0", "k1")]
    + [("w", "c", "g0", "g1")] * 3
    + [("w", "c", "c", "g0", "g1"), ("k0",)]
    + [("w", "r0")] * 3
    + [("k1", "w", "r0"), ("w", "r0"), ("k1", "w", "r0", "r1")]
    + [("r0", "r1")] * 2
    + [("w", "r0", "r1"), ("r0", "r1"), ("r1",), ("w",), ("r1",)]
)
YN = 4
CUTS = 4


def shifted(x, axis, by):
    count = lax.axis_size(axis)
    pairs = [(i, i + by) for i in range(count) if 0 <= i + by < count]
    return lax.ppermute(x, axis, pairs)


def layer_kernel(
    zn,
    blocks,
    code_ref,
    q_ref,
    k_ref,
    v_ref,
    w_ref,
    residual_ref,
    drop_ref,
    gain_ref,
    bias_ref,
    next_ref,
    normed_ref,
    *scratch,
):
    groups = q_ref.shape[0]
    span = q_ref.shape[3] // GROUP
    wide = GROUP * HEAD
    rows = k_ref.shape[0]
    me = lax.axis_index("dp")
    tens = lax.axis_index("tensor")
    z, x = me // XN, me % XN
    z_up = ((z + 1) % zn) * XN + x
    z_dn = ((z + zn - 1) % zn) * XN + x
    x_up = z * XN + (x + 1) % XN
    x_dn = z * XN + (x + XN - 1) % XN
    devices = zn * XN
    d_next = (me + 1) % devices
    d_prev = (me + devices - 1) % devices
    y, core = tens // 2, tens % 2
    y_up = ((y + 1) % YN) * 2 + core
    y_dn = ((y + YN - 1) % YN) * 2 + core
    partner = y * 2 + 1 - core
    per_g = 7
    bufs = [scratch[g * per_g : (g + 1) * per_g] for g in range(groups)]
    (
        codes,
        table,
        slots,
        code_send,
        code_recv,
        ag_send,
        ag_recv,
        kv_own,
        kv_send,
        kv_recv,
        rd_send,
        rd_recv,
        rs_send,
        rs_recv,
        table_sem,
        weight,
        merged,
        rows_f32,
        sums,
        a_out,
        a_in,
        far_out,
        far_in,
        near_out,
        near_in,
        w_send,
        w_recv,
        wx_send,
        wx_recv,
        h_send,
        h_recv,
        a_send,
        a_recv,
        b_send,
        b_recv,
    ) = scratch[groups * per_g :]
    far, near = zn // 2, zn // 2 - 1
    chains = [
        (way, b, far if (b < blocks // 2) == (way > 0) else near)
        for b in range(blocks)
        for way in (1, -1)
    ]
    started = []

    barrier = pltpu.get_barrier_semaphore()
    for peer in (z_up, z_dn, x_up, x_dn, d_next, d_prev):
        pl.semaphore_signal(barrier, inc=1, device_id=(peer, tens), device_id_type=MESH)
    for peer in (y_up, y_dn, partner):
        pl.semaphore_signal(barrier, inc=1, device_id=(me, peer), device_id_type=MESH)
    pl.semaphore_wait(barrier, 9)

    def copy_to(src, dst, send, recv, peer):
        return pltpu.make_async_remote_copy(
            src_ref=src,
            dst_ref=dst,
            send_sem=send,
            recv_sem=recv,
            device_id=peer if isinstance(peer, tuple) else (peer, tens),
            device_id_type=MESH,
        )

    def remote(src, dst, send, recv, peer):
        copy = copy_to(src, dst, send, recv, peer)
        copy.start()
        started.append(copy)
        return copy

    def stores(g):
        hb = rows // 2
        lo, hi = pl.ds(0, hb), pl.ds(hb, hb)
        cols = pl.ds(g * wide, wide)
        pairs = [(k_ref, bufs[g][1]), (v_ref, bufs[g][2])]
        own, first, later = [], [], []
        for n, (src, dst) in enumerate(pairs):
            whole = src.at[:, :, cols] if n == 0 else src.at[:, g]
            copy = pltpu.make_async_copy(whole, dst.at[0], kv_own.at[g, n])
            copy.start()
            own.append(copy)
        for part, place, peer, at in ((lo, 3, x_up, 0), (hi, 1, x_dn, 1), (hi, 3, x_up, 2), (lo, 1, x_dn, 3)):
            for n, (src, dst) in enumerate(pairs):
                copy = remote(
                    src.at[part, :, cols] if n == 0 else src.at[part, g],
                    dst.at[place, part],
                    kv_send.at[g, n, at],
                    kv_recv.at[g, n, at],
                    peer,
                )
                (first if at < 2 else later).append(copy)
        yield
        for i, (part, place, peer, at) in enumerate(((lo, 3, x_up, 4), (hi, 1, x_dn, 5))):
            for n, (_, dst) in enumerate(pairs):
                first[2 * i + n].wait_recv()
                later.append(
                    remote(
                        dst.at[place, part],
                        dst.at[2, part],
                        kv_send.at[g, n, at],
                        kv_recv.at[g, n, at],
                        peer,
                    )
                )
        yield
        for copy in own:
            copy.wait()
        for copy in later:
            copy.wait_recv()
        yield

    def gather_codes():
        codes[z] = code_ref[...]
        for s in range(far + 1):
            for c, (way, steps) in enumerate(((1, far), (-1, near))):
                if s > steps:
                    continue
                here = codes.at[(z - way * s + zn) % zn]
                peer = z_up if way > 0 else z_dn
                if s > 0:
                    copy_to(here, here, code_send.at[c, s - 1], code_recv.at[c, s - 1], peer).wait_recv()
                if s < steps:
                    src = code_ref if s == 0 else here
                    remote(src, here, code_send.at[c, s], code_recv.at[c, s], peer)
            yield
        copy = pltpu.make_async_copy(codes, table, table_sem)
        copy.start()
        copy.wait()

        @pl.loop(0, zn)
        def _(z0):
            asks = [table[z0, 0, k] for k in range(2 * blocks)]
            for r in range(XN):
                first = (z * XN + (x + r) % XN) * rows
                block, at = jnp.int32(0), jnp.int32(0)
                for k, ask in enumerate(asks):
                    hit = (ask >= first) & (ask < first + rows)
                    block = jnp.where(hit, k // 2, block)
                    at = jnp.where(hit, ask - first, at)
                slots[z0, r] = z0 * blocks + block
                slots[z0, XN + r] = at
            for k, ask in enumerate(asks):
                holder = ask // rows
                there = holder // XN == z
                slots[z0, 2 * XN + k] = jnp.where(there, (holder - x + XN) % XN, XN)

        yield

    def gather(g):
        col = bufs[g][0]
        for b in range(blocks):
            col[z * blocks + b] = q_ref[g, b]
        for s in range(far + 1):
            for c, (way, block, steps) in enumerate(chains):
                if s > steps:
                    continue
                here = col.at[((z - way * s + zn) % zn) * blocks + block]
                peer = z_up if way > 0 else z_dn
                if s > 0:
                    copy_to(
                        here, here, ag_send.at[g, c, s - 1], ag_recv.at[g, c, s - 1], peer
                    ).wait_recv()
                if s < steps:
                    src = q_ref.at[g, block] if s == 0 else here
                    remote(src, here, ag_send.at[g, c, s], ag_recv.at[g, c, s], peer)
            yield

    left = lax.broadcasted_iota(jnp.int32, (HEAD, GROUP * span), 1) < span
    left_bf = left.astype(jnp.float32).astype(jnp.bfloat16)
    right_bf = (1.0 - left.astype(jnp.float32)).astype(jnp.bfloat16)

    def attend(g, z0):
        col, keys, values, res, stat = bufs[g][:5]
        scale = HEAD ** (-0.5)
        for pair in range(0, XN, 2):
            places = (pair, pair + 1)
            at = [slots[z0, XN + r] for r in places]
            scores = []
            for r, a in zip(places, at):
                q = col[slots[z0, r]]
                q2 = jnp.concatenate([q * left_bf, q * right_bf], axis=0)
                scores.append(jnp.dot(keys[r, a], q2, preferred_element_type=jnp.float32))
            tops = [jnp.max(v, axis=0, keepdims=True) for v in scores]
            raised = [jnp.exp((v - t) * scale) for v, t in zip(scores, tops)]
            totals = [jnp.sum(v, axis=0, keepdims=True) for v in raised]
            for r, a, e, top, total in zip(places, at, raised, tops, totals):
                eb = e.astype(jnp.bfloat16)
                p2 = jnp.concatenate([eb * left_bf, eb * right_bf], axis=0)
                part = jnp.dot(values[r, a], p2, preferred_element_type=jnp.float32)
                res[z0 * XN + r] = (part * (1.0 / total)).astype(jnp.bfloat16)
                stat[z0, r : r + 1, :] = top * scale + jnp.log(total)
        stat[z0, XN : XN + 1, :] = jnp.full((1, GROUP * span), NONE, jnp.float32)

    def combine(g, z0, block, arrived, dst, dst_stat):
        res, stat = bufs[g][3:5]
        lses = [ref[...] for _, ref in arrived]
        vals = [ref[...] for ref, _ in arrived]
        for r in range(2):
            place = slots[z0, 2 * XN + 2 * block + r]
            lses.append(stat[z0, pl.ds(place, 1), :])
            vals.append(res[z0 * XN + jnp.minimum(place, XN - 1)])
        top = functools.reduce(jnp.maximum, lses)
        weights = [jnp.exp(v - top) for v in lses]
        total = functools.reduce(jnp.add, weights)
        if dst_stat is not None:
            dst_stat[...] = top + jnp.log(total)
        share = 1.0 / total
        acc = vals[0].astype(jnp.float32) * (weights[0] * share)
        for v, w in zip(vals[1:], weights[1:]):
            acc += v.astype(jnp.float32) * (w * share)
        dst[...] = acc.astype(jnp.bfloat16)

    def reduce(g):
        ring, ring_stat = bufs[g][5:7]
        attend(g, (z + far) % zn)
        for s in range(far + 1):
            for c, (way, block, steps) in enumerate(chains):
                i = s - (far - steps)
                if i < 0 or i > steps:
                    continue
                here, here_stat = ring.at[c, i], ring_stat.at[c, i, pl.ds(0, 1)]
                peer = z_up if way > 0 else z_dn
                if i > 0:
                    for ref, snd, rcv in (
                        (here, rd_send, rd_recv),
                        (here_stat, rs_send, rs_recv),
                    ):
                        copy_to(
                            ref, ref, snd.at[g, c, i - 1], rcv.at[g, c, i - 1], peer
                        ).wait_recv()
                if i < steps:
                    z0 = (z + way * (steps - i) + zn) % zn
                    arrived = [(here, here_stat)] if i > 0 else []
                    combine(g, z0, block, arrived, here, here_stat)
                    remote(
                        here_stat,
                        ring_stat.at[c, i + 1, pl.ds(0, 1)],
                        rs_send.at[g, c, i],
                        rs_recv.at[g, c, i],
                        peer,
                    )
                    remote(
                        here,
                        ring.at[c, i + 1],
                        rd_send.at[g, c, i],
                        rd_recv.at[g, c, i],
                        peer,
                    )
            away = far - (s + 1)
            if away > 0:

                @pl.loop(0, 2)
                def _(n):
                    attend(g, (z + (1 - 2 * n) * away + zn) % zn)

            elif away == 0:
                attend(g, z)
            yield
        for b in range(blocks):
            arrived = [
                (ring.at[c, steps], ring_stat.at[c, steps, pl.ds(0, 1)])
                for c, (_, block, steps) in enumerate(chains)
                if block == b
            ]
            combine(g, z, b, arrived, merged.at[g, b], None)
            turned = jnp.transpose(merged[g, b].astype(jnp.float32))
            for h in range(GROUP):
                at = (g * GROUP + h) * HEAD
                rows_f32[b * span : (b + 1) * span, at : at + HEAD] = turned[
                    h * span : (h + 1) * span
                ]
        cols = pl.ds(g * wide, wide)
        halo.append(
            remote(
                rows_f32.at[pl.ds(0, 8), cols],
                rows_f32.at[pl.ds(blocks * span, 8), cols],
                h_send.at[g],
                h_recv.at[g],
                d_prev,
            )
        )
        yield

    def gather_weight():
        weight[z, x] = w_ref[...]
        for s in range(far + 1):
            for c, (way, steps) in enumerate(((1, far), (-1, near))):
                if s > steps:
                    continue
                here = weight.at[(z - way * s + zn) % zn, x]
                peer = z_up if way > 0 else z_dn
                if s > 0:
                    copy_to(here, here, w_send.at[c, s - 1], w_recv.at[c, s - 1], peer).wait_recv()
                if s < steps:
                    src = w_ref if s == 0 else here
                    remote(src, here, w_send.at[c, s], w_recv.at[c, s], peer)
            yield
        lo, hi = pl.ds(0, zn // 2), pl.ds(zn // 2, zn // 2)

        def send(part, column, peer, at):
            here = weight.at[part, column]
            return remote(here, here, wx_send.at[at], wx_recv.at[at], peer)

        first = [send(lo, x, x_up, 0), send(hi, x, x_dn, 1)]
        later = [send(hi, x, x_up, 2), send(lo, x, x_dn, 3)]
        yield
        first[0].wait_recv()
        later.append(send(lo, (x + XN - 1) % XN, x_up, 4))
        first[1].wait_recv()
        later.append(send(hi, (x + 1) % XN, x_dn, 5))
        yield
        for copy in later:
            copy.wait_recv()
        yield

    def project():
        total = blocks * span
        width = next_ref.shape[1]
        depth = rows_f32.shape[1]
        own = total // (2 * YN)
        cut = width // CUTS
        zs = zn // CUTS
        half = own // 2
        up, dn, op = (y + 1) % YN, (y + YN - 1) % YN, (y + 2) % YN
        lo, hi = pl.ds(0, half), pl.ds(half, half)
        for copy in halo:
            copy.wait_recv()
        cross = rows_f32[1 : total + 1, :]
        ends = lax.broadcasted_iota(jnp.int32, (total, depth), 0) == total - 1
        cross = jnp.where(ends & (me == devices - 1), 0.0, cross).astype(jnp.bfloat16)
        a_copy, opposite, lone, shared = [], [], [], []
        for n in range(CUTS):
            for i in range(zs):
                part = weight[n * zs + i].reshape(width // zn, depth)
                product = lax.dot_general(
                    cross, part, (((1,), (1,)), ((), ())), preferred_element_type=jnp.float32
                )
                at = n * cut + i * (width // zn)
                sums[:, :, at : at + width // zn] = product.reshape(2 * YN, own, width // zn)
            cols = slice(n * cut, (n + 1) * cut)
            for other in range(YN):
                a_out[n, other] = sums[other * 2 + 1 - core, :, cols].astype(jnp.bfloat16)
            a_copy.append(
                remote(a_out.at[n], a_in.at[n], a_send.at[n], a_recv.at[n], (me, partner))
            )

        def send(src, dst, n, at, peer):
            return remote(src, dst, b_send.at[n, at], b_recv.at[n, at], (me, peer))

        def chip_sum(n):
            cols = slice(n * cut, (n + 1) * cut)
            a_copy[n].wait_recv()
            for other in range(YN):
                sums[other * 2 + core, :, cols] += a_in[n, other].astype(jnp.float32)
            far_out[n] = sums[op * 2 + core, :, cols].astype(jnp.bfloat16)
            opposite.append(
                (
                    send(far_out.at[n, lo], far_in.at[n, lo], n, 0, y_up),
                    send(far_out.at[n, hi], far_in.at[n, hi], n, 1, y_dn),
                )
            )
            near_out[n, 0, half:, :] = sums[up * 2 + core, half:, cols].astype(jnp.bfloat16)
            near_out[n, 1, :half, :] = sums[dn * 2 + core, :half, cols].astype(jnp.bfloat16)
            lone.append(
                (
                    send(near_out.at[n, 0, hi], near_in.at[n, 0, hi], n, 2, y_up),
                    send(near_out.at[n, 1, lo], near_in.at[n, 1, lo], n, 3, y_dn),
                )
            )

        def pass_on(n):
            cols = slice(n * cut, (n + 1) * cut)
            for copy in opposite[n]:
                copy.wait_recv()
            mine = sums[up * 2 + core, :half, cols] + far_in[n, :half, :].astype(jnp.float32)
            near_out[n, 0, :half, :] = mine.astype(jnp.bfloat16)
            mine = sums[dn * 2 + core, half:, cols] + far_in[n, half:, :].astype(jnp.float32)
            near_out[n, 1, half:, :] = mine.astype(jnp.bfloat16)
            shared.append(
                (
                    send(near_out.at[n, 0, lo], near_in.at[n, 0, lo], n, 4, y_up),
                    send(near_out.at[n, 1, hi], near_in.at[n, 1, hi], n, 5, y_dn),
                )
            )

        def stream(n):
            cols = slice(n * cut, (n + 1) * cut)
            for copy in lone[n] + shared[n]:
                copy.wait_recv()
            branch = sums[tens, :, cols]
            for side in range(2):
                branch += near_in[n, side].astype(jnp.float32)
            keep = drop_ref[:, cols].astype(jnp.float32) * (1.0 / keep_rate)
            value = residual_ref[:, cols].astype(jnp.float32) + keep * branch
            sums[tens, :, cols] = value
            next_ref[:, cols] = value.astype(jnp.bfloat16)
            return jnp.sum(value, axis=1, keepdims=True)

        tally = jnp.zeros((own, 1), jnp.float32)
        for n in range(CUTS + 2):
            if n < CUTS:
                chip_sum(n)
            if 1 <= n <= CUTS:
                pass_on(n - 1)
            if n >= 2:
                tally += stream(n - 2)
        centre = tally / width
        spread = jnp.zeros((own, 1), jnp.float32)
        for at in range(0, width, cut):
            off = sums[tens, :, at : at + cut] - centre
            spread += jnp.sum(off * off, axis=1, keepdims=True)
        scale = lax.rsqrt(spread / width + norm_eps)
        for at in range(0, width, cut):
            cols = slice(at, at + cut)
            normed = (sums[tens, :, cols] - centre) * scale * gain_ref[:, cols] + bias_ref[:, cols]
            normed_ref[:, cols] = normed.astype(jnp.bfloat16)

    halo = []
    live = {"c": gather_codes(), "w": gather_weight()}
    parts = {"g": gather, "k": stores, "r": reduce}
    for step in ORDER:
        for name in step:
            if name not in live:
                live[name] = parts[name[0]](int(name[1:]))
            next(live[name], None)
    for it in live.values():
        for _ in it:
            pass
    project()
    for copy in started:
        copy.wait_send()


def layer(code, q, k, v, weight, residual, drop, gain, bias):
    groups, blocks, deep, wide = q.shape
    rows = k.shape[0]
    zn = lax.axis_size("dp") // XN
    steps = zn // 2
    bf, f32 = jnp.bfloat16, jnp.float32
    own, width = residual.shape
    depth = weight.shape[1]
    cut = width // CUTS
    span = wide // GROUP
    per_group = [
        pltpu.VMEM((zn * blocks, deep, wide), bf),
        pltpu.VMEM((XN, rows, k.shape[1], GROUP * HEAD), bf),
        pltpu.VMEM((XN, rows) + v.shape[2:], bf),
        pltpu.VMEM((zn * XN, deep, wide), bf),
        pltpu.VMEM((zn, 8, wide), f32),
        pltpu.VMEM((2 * blocks, steps + 1, deep, wide), bf),
        pltpu.VMEM((2 * blocks, steps + 1, 8, wide), f32),
    ]
    dma = pltpu.SemaphoreType.DMA
    vmem = pl.BlockSpec(memory_space=pltpu.VMEM)
    hbm = pl.BlockSpec(memory_space=pl.ANY)
    ring = dma((groups, 2 * blocks, steps))
    return pl.pallas_call(
        functools.partial(layer_kernel, zn, blocks),
        out_shape=[jax.ShapeDtypeStruct(residual.shape, bf)] * 2,
        in_specs=[vmem, vmem, hbm, hbm] + [vmem] * 5,
        out_specs=[vmem, vmem],
        scratch_shapes=per_group * groups
        + [
            pltpu.VMEM((zn, 8, HEAD), jnp.int32),
            pltpu.SMEM((zn, 8, HEAD), jnp.int32),
            pltpu.SMEM((zn, 2 * XN + 2 * blocks), jnp.int32),
            dma((2, steps)),
            dma((2, steps)),
            ring,
            ring,
            dma((groups, 2)),
            dma((groups, 2, 6)),
            dma((groups, 2, 6)),
            ring,
            ring,
            ring,
            ring,
            dma,
            pltpu.VMEM((zn, XN) + weight.shape, bf),
            pltpu.VMEM((groups, blocks, deep, wide), bf),
            pltpu.VMEM((blocks * span + 8, depth), f32),
            pltpu.VMEM((2 * YN, own, width), f32),
            pltpu.VMEM((CUTS, YN, own, cut), bf),
            pltpu.VMEM((CUTS, YN, own, cut), bf),
            pltpu.VMEM((CUTS, own, cut), bf),
            pltpu.VMEM((CUTS, own, cut), bf),
            pltpu.VMEM((CUTS, 2, own, cut), bf),
            pltpu.VMEM((CUTS, 2, own, cut), bf),
            dma((2, steps)),
            dma((2, steps)),
            dma((6,)),
            dma((6,)),
            dma((groups,)),
            dma((groups,)),
            dma((CUTS,)),
            dma((CUTS,)),
            dma((CUTS, 6)),
            dma((CUTS, 6)),
        ],
        compiler_params=pltpu.CompilerParams(
            collective_id=0, has_side_effects=True, vmem_limit_bytes=56 * 1024 * 1024
        ),
        cost_estimate=pl.CostEstimate(
            flops=2_200_000_000, bytes_accessed=6_000_000, transcendentals=2_200_000
        ),
    )(code, q, k, v, weight, residual, drop, gain, bias)


def local(
    queries,
    neighbour_keys,
    neighbour_values,
    residual,
    out_weight,
    drop_mask,
    norm_gain,
    norm_bias,
    neighbour_owner,
    neighbour_slot,
):
    row_width = queries.shape[1]
    blocks = neighbour_owner.shape[0]
    span = queries.shape[0] // blocks
    groups = row_width // (GROUP * HEAD)
    code = (neighbour_owner * neighbour_keys.shape[0] + neighbour_slot).reshape(1, -1)
    code = jnp.pad(code, ((0, 7), (0, HEAD - code.shape[1])))
    carried = shifted(queries[-1:], "dp", 1)
    asked = jnp.concatenate([carried, queries[:-1]], axis=0)
    asked = asked.reshape(blocks, span, groups, GROUP, HEAD).transpose(2, 0, 4, 3, 1)
    asked = asked.reshape(groups, blocks, HEAD, GROUP * span)
    rows, length, _ = neighbour_values.shape
    values = neighbour_values.reshape(rows, length, groups, GROUP, HEAD).transpose(0, 2, 4, 3, 1)
    values = values.reshape(rows, groups, HEAD, GROUP * length)
    return tuple(
        layer(
            code,
            asked,
            neighbour_keys,
            values,
            out_weight.T,
            residual,
            drop_mask,
            norm_gain.reshape(1, -1),
            norm_bias.reshape(1, -1),
        )
    )


def solution(mesh):
    placed = (
        P("dp", "tensor"),
        P("dp", None, "tensor"),
        P("dp", None, "tensor"),
        P(("dp", "tensor"), None),
        P("tensor", "dp"),
        P(("dp", "tensor"), None),
        P(),
        P(),
        P("dp", None),
        P("dp", None),
    )
    return jax.shard_map(
        local,
        mesh=mesh,
        in_specs=placed,
        out_specs=(P(("dp", "tensor"), None), P(("dp", "tensor"), None)),
        check_vma=False,
    )
```

```python
import functools

import jax
import jax.numpy as jnp
from jax import lax
from jax.experimental import pallas as pl
from jax.experimental.pallas import tpu as pltpu
from jax.sharding import PartitionSpec as P

HEAD = 128
XN = 4
GROUP = 2
NONE = -1e30

keep_rate = 0.9
norm_eps = 1e-05
MESH = pl.DeviceIdType.MESH


ORDER = (
    [("k0", "c", "g0", "g1")]
    + [("c", "g0", "g1")] * 3
    + [("c", "g0", "g1", "k0", "k1")]
    + [("w", "c", "g0", "g1")] * 3
    + [("w", "c", "c", "g0", "g1"), ("k0",)]
    + [("w", "r0")] * 3
    + [("k1", "w", "r0"), ("w", "r0"), ("k1", "w", "r0", "r1")]
    + [("r0", "r1")] * 2
    + [("w", "r0", "r1"), ("r0", "r1"), ("r1",), ("w",), ("r1",)]
)
YN = 4
CUTS = 4


def shifted(x, axis, by):
    count = lax.axis_size(axis)
    pairs = [(i, i + by) for i in range(count) if 0 <= i + by < count]
    return lax.ppermute(x, axis, pairs)


def layer_kernel(
    zn,
    blocks,
    code_ref,
    q_ref,
    k_ref,
    v_ref,
    w_ref,
    residual_ref,
    drop_ref,
    gain_ref,
    bias_ref,
    next_ref,
    normed_ref,
    *scratch,
):
    groups = q_ref.shape[0]
    span = q_ref.shape[3] // GROUP
    wide = GROUP * HEAD
    rows = k_ref.shape[0]
    me = lax.axis_index("dp")
    tens = lax.axis_index("tensor")
    z, x = me // XN, me % XN
    z_up = ((z + 1) % zn) * XN + x
    z_dn = ((z + zn - 1) % zn) * XN + x
    x_up = z * XN + (x + 1) % XN
    x_dn = z * XN + (x + XN - 1) % XN
    devices = zn * XN
    d_next = (me + 1) % devices
    d_prev = (me + devices - 1) % devices
    y, core = tens // 2, tens % 2
    y_up = ((y + 1) % YN) * 2 + core
    y_dn = ((y + YN - 1) % YN) * 2 + core
    partner = y * 2 + 1 - core
    per_g = 7
    bufs = [scratch[g * per_g : (g + 1) * per_g] for g in range(groups)]
    (
        codes,
        table,
        slots,
        code_send,
        code_recv,
        ag_send,
        ag_recv,
        kv_own,
        kv_send,
        kv_recv,
        rd_send,
        rd_recv,
        rs_send,
        rs_recv,
        table_sem,
        weight,
        own_stat,
        rows_f32,
        sums,
        a_out,
        a_in,
        far_out,
        far_in,
        near_out,
        near_in,
        w_send,
        w_recv,
        wx_send,
        wx_recv,
        h_send,
        h_recv,
        a_send,
        a_recv,
        b_send,
        b_recv,
    ) = scratch[groups * per_g :]
    far, near = zn // 2, zn // 2 - 1
    hb = blocks // 2
    chains = [
        (way, half, far if (half == 0) == (way > 0) else near)
        for half in range(2)
        for way in (1, -1)
    ]
    started, pending = [], {}

    barrier = pltpu.get_barrier_semaphore()
    for peer in (z_up, z_dn, x_up, x_dn, d_next, d_prev):
        pl.semaphore_signal(barrier, inc=1, device_id=(peer, tens), device_id_type=MESH)
    for peer in (y_up, y_dn, partner):
        pl.semaphore_signal(barrier, inc=1, device_id=(me, peer), device_id_type=MESH)
    pl.semaphore_wait(barrier, 9)

    def copy_to(src, dst, send, recv, peer):
        return pltpu.make_async_remote_copy(
            src_ref=src,
            dst_ref=dst,
            send_sem=send,
            recv_sem=recv,
            device_id=peer if isinstance(peer, tuple) else (peer, tens),
            device_id_type=MESH,
        )

    def remote(src, dst, send, recv, peer, key=None):
        copy = copy_to(src, dst, send, recv, peer)
        if key in pending:
            pending.pop(key).wait_send()
        copy.start()
        if key is None:
            started.append(copy)
        else:
            pending[key] = copy
        return copy

    def stores(g):
        hb = rows // 2
        lo, hi = pl.ds(0, hb), pl.ds(hb, hb)
        cols = pl.ds(g * wide, wide)
        pairs = [(k_ref, bufs[g][1]), (v_ref, bufs[g][2])]
        own, first, later = [], [], []
        for n, (src, dst) in enumerate(pairs):
            whole = src.at[:, :, cols] if n == 0 else src.at[:, cols]
            copy = pltpu.make_async_copy(whole, dst.at[0], kv_own.at[g, n])
            copy.start()
            own.append(copy)
        for part, place, peer, at in ((lo, 3, x_up, 0), (hi, 1, x_dn, 1), (hi, 3, x_up, 2), (lo, 1, x_dn, 3)):
            for n, (src, dst) in enumerate(pairs):
                copy = remote(
                    src.at[part, :, cols] if n == 0 else src.at[part, cols],
                    dst.at[place, part],
                    kv_send.at[g, n, at],
                    kv_recv.at[g, n, at],
                    peer,
                )
                (first if at < 2 else later).append(copy)
        yield
        for i, (part, place, peer, at) in enumerate(((lo, 3, x_up, 4), (hi, 1, x_dn, 5))):
            for n, (_, dst) in enumerate(pairs):
                first[2 * i + n].wait_recv()
                later.append(
                    remote(
                        dst.at[place, part],
                        dst.at[2, part],
                        kv_send.at[g, n, at],
                        kv_recv.at[g, n, at],
                        peer,
                    )
                )
        yield
        for copy in own:
            copy.wait()
        for copy in later:
            copy.wait_recv()
        yield

    def gather_codes():
        codes[z] = code_ref[...]
        for s in range(far + 1):
            for c, (way, steps) in enumerate(((1, far), (-1, near))):
                if s > steps:
                    continue
                here = codes.at[(z - way * s + zn) % zn]
                peer = z_up if way > 0 else z_dn
                if s > 0:
                    copy_to(here, here, code_send.at[c, 0], code_recv.at[c, s - 1], peer).wait_recv()
                if s < steps:
                    src = code_ref if s == 0 else here
                    remote(src, here, code_send.at[c, s % 2], code_recv.at[c, s], peer, ("c", c, s % 2))
            yield
        copy = pltpu.make_async_copy(codes, table, table_sem)
        copy.start()
        copy.wait()

        @pl.loop(0, zn)
        def _(z0):
            asks = [table[z0, 0, k] for k in range(2 * blocks)]
            for r in range(XN):
                first = (z * XN + (x + r) % XN) * rows
                block, at = jnp.int32(0), jnp.int32(0)
                for k, ask in enumerate(asks):
                    hit = (ask >= first) & (ask < first + rows)
                    block = jnp.where(hit, k // 2, block)
                    at = jnp.where(hit, ask - first, at)
                slots[z0, r] = z0 * blocks + block
                slots[z0, XN + r] = at
            for k, ask in enumerate(asks):
                holder = ask // rows
                there = holder // XN == z
                slots[z0, 2 * XN + k] = jnp.where(there, (holder - x + XN) % XN, XN)

        yield

    def gather(g):
        col = bufs[g][0]
        for b in range(blocks):
            col[z * blocks + b] = q_ref[g, b]
        for s in range(far + 1):
            for c, (way, half, steps) in enumerate(chains):
                if s > steps:
                    continue
                at = ((z - way * s + zn) % zn) * blocks + half * hb
                here = col.at[pl.ds(at, hb)]
                peer = z_up if way > 0 else z_dn
                if s > 0:
                    copy_to(
                        here, here, ag_send.at[g, c, 0], ag_recv.at[g, c, s - 1], peer
                    ).wait_recv()
                if s < steps:
                    src = q_ref.at[g, pl.ds(half * hb, hb)] if s == 0 else here
                    remote(
                        src,
                        here,
                        ag_send.at[g, c, s % 2],
                        ag_recv.at[g, c, s],
                        peer,
                        ("g", g, c, s % 2),
                    )
            yield

    left = lax.broadcasted_iota(jnp.int32, (HEAD, GROUP * span), 1) < span
    left_bf = left.astype(jnp.float32).astype(jnp.bfloat16)
    right_bf = (1.0 - left.astype(jnp.float32)).astype(jnp.bfloat16)

    def attend(g, z0):
        col, keys, values, res, stat = bufs[g][:5]
        scale = HEAD ** (-0.5)
        for pair in range(0, XN, 2):
            places = (pair, pair + 1)
            at = [slots[z0, XN + r] for r in places]
            scores = []
            for r, a in zip(places, at):
                q = col[slots[z0, r]]
                q2 = jnp.concatenate([q * left_bf, q * right_bf], axis=0)
                scores.append(jnp.dot(keys[r, a], q2, preferred_element_type=jnp.float32))
            tops = [jnp.max(v, axis=0, keepdims=True) for v in scores]
            raised = [jnp.exp((v - t) * scale) for v, t in zip(scores, tops)]
            totals = [jnp.sum(v, axis=0, keepdims=True) for v in raised]
            for r, a, e, top, total in zip(places, at, raised, tops, totals):
                eb = e.astype(jnp.bfloat16)
                p2 = jnp.concatenate([eb * left_bf, eb * right_bf], axis=0)
                v = values[r, a]
                v2 = jnp.concatenate([v[:HEAD], v[HEAD:]], axis=1)
                part = jnp.dot(v2, p2, preferred_element_type=jnp.float32)
                res[z0 * XN + r] = (part * (1.0 / total)).astype(jnp.bfloat16)
                stat[z0, r : r + 1, :] = top * scale + jnp.log(total)
        stat[z0, XN : XN + 1, :] = jnp.full((1, GROUP * span), NONE, jnp.float32)

    block_row = lax.broadcasted_iota(jnp.int32, (8, GROUP * span), 0)

    def shares(g, z0, arrived, spare):
        stat = bufs[g][4]
        for r in range(2):
            for b in range(blocks):
                place = slots[z0, 2 * XN + 2 * b + r]
                own_stat[spare + r, b : b + 1, :] = stat[z0, pl.ds(place, 1), :]
        lses = arrived + [own_stat[spare], own_stat[spare + 1]]
        top = functools.reduce(jnp.maximum, lses)
        weights = [jnp.exp(v - top) for v in lses]
        total = functools.reduce(jnp.add, weights)
        return [w / total for w in weights], top + jnp.log(total)

    def combine(g, z0, block, arrived, weights):
        res = bufs[g][3]
        vals = list(arrived)
        for r in range(2):
            place = slots[z0, 2 * XN + 2 * block + r]
            vals.append(res[z0 * XN + jnp.minimum(place, XN - 1)])
        parts = [
            v.astype(jnp.float32) * w[block : block + 1] for v, w in zip(vals, weights)
        ]
        return functools.reduce(jnp.add, parts).astype(jnp.bfloat16)

    def reduce(g):
        ring, ring_stat = bufs[g][5:7]
        for n in range(4):
            own_stat[4 * g + n] = jnp.full((8, GROUP * span), NONE, jnp.float32)
        attend(g, (z + far) % zn)
        for s in range(far):
            ways = []
            for w, way in enumerate((1, -1)):
                peer = z_up if way > 0 else z_dn
                here = ring_stat.at[w, s]
                arrived = []
                if s > 0:
                    copy_to(
                        here, here, rs_send.at[g, w, 0], rs_recv.at[g, w, s - 1], peer
                    ).wait_recv()
                    arrived = [here[...]]
                z0 = (z + way * (far - s) + zn) % zn
                weights, lse = shares(g, z0, arrived, 4 * g + 2 * w)
                if s == 0:
                    mine = (block_row < hb) == (way > 0)
                    lse = jnp.where(mine, lse, NONE)
                here[...] = lse
                remote(
                    here,
                    ring_stat.at[w, s + 1],
                    rs_send.at[g, w, s % 2],
                    rs_recv.at[g, w, s],
                    peer,
                    ("s", g, w, s % 2),
                )
                ways.append((z0, weights))
            for c, (way, half, steps) in enumerate(chains):
                i = s - (far - steps)
                if i < 0:
                    continue
                here = ring.at[c, i]
                peer = z_up if way > 0 else z_dn
                z0, weights = ways[0 if way > 0 else 1]
                if i > 0:
                    copy_to(
                        here, here, rd_send.at[g, c, 0], rd_recv.at[g, c, i - 1], peer
                    ).wait_recv()
                for b in range(hb):
                    arrived = [here[b]] if i > 0 else []
                    here[b] = combine(
                        g, z0, half * hb + b, arrived, weights[len(weights) - 2 - len(arrived) :]
                    )
                remote(
                    here,
                    ring.at[c, i + 1],
                    rd_send.at[g, c, i % 2],
                    rd_recv.at[g, c, i],
                    peer,
                    ("d", g, c, i % 2),
                )
            away = far - (s + 1)
            if away > 0:

                @pl.loop(0, 2)
                def _(n):
                    attend(g, (z + (1 - 2 * n) * away + zn) % zn)

            else:
                attend(g, z)
            yield
        arrived = []
        for w, peer in enumerate((z_up, z_dn)):
            here = ring_stat.at[w, far]
            copy_to(
                here, here, rs_send.at[g, w, 0], rs_recv.at[g, w, far - 1], peer
            ).wait_recv()
            arrived.append(here[...])
        weights, _ = shares(g, z, arrived, 4 * g)
        for c, (way, half, steps) in enumerate(chains):
            here = ring.at[c, steps]
            peer = z_up if way > 0 else z_dn
            copy_to(
                here, here, rd_send.at[g, c, 0], rd_recv.at[g, c, steps - 1], peer
            ).wait_recv()
        for b in range(blocks):
            half = b // hb
            arrived = [ring[2 * half + w, chains[2 * half + w][2], b % hb] for w in range(2)]
            rows = combine(g, z, b, arrived, weights)
            turned = jnp.transpose(rows.astype(jnp.float32))
            for h in range(GROUP):
                at = (g * GROUP + h) * HEAD
                rows_f32[b * span : (b + 1) * span, at : at + HEAD] = turned[
                    h * span : (h + 1) * span
                ]
        cols = pl.ds(g * wide, wide)
        halo.append(
            remote(
                rows_f32.at[pl.ds(0, 8), cols],
                rows_f32.at[pl.ds(blocks * span, 8), cols],
                h_send.at[g],
                h_recv.at[g],
                d_prev,
            )
        )
        yield

    def gather_weight():
        weight[z, x] = w_ref[...]
        for s in range(far + 1):
            for c, (way, steps) in enumerate(((1, far), (-1, near))):
                if s > steps:
                    continue
                here = weight.at[(z - way * s + zn) % zn, x]
                peer = z_up if way > 0 else z_dn
                if s > 0:
                    copy_to(here, here, w_send.at[c, 0], w_recv.at[c, s - 1], peer).wait_recv()
                if s < steps:
                    src = w_ref if s == 0 else here
                    remote(src, here, w_send.at[c, s % 2], w_recv.at[c, s], peer, ("w", c, s % 2))
            yield
        lo, hi = pl.ds(0, zn // 2), pl.ds(zn // 2, zn // 2)

        def send(part, column, peer, at):
            here = weight.at[part, column]
            return remote(here, here, wx_send.at[at], wx_recv.at[at], peer)

        first = [send(lo, x, x_up, 0), send(hi, x, x_dn, 1)]
        later = [send(hi, x, x_up, 2), send(lo, x, x_dn, 3)]
        yield
        first[0].wait_recv()
        later.append(send(lo, (x + XN - 1) % XN, x_up, 4))
        first[1].wait_recv()
        later.append(send(hi, (x + 1) % XN, x_dn, 5))
        yield
        for copy in later:
            copy.wait_recv()
        yield

    def project():
        total = blocks * span
        width = next_ref.shape[1]
        depth = rows_f32.shape[1]
        own = total // (2 * YN)
        cut = width // CUTS
        zs = zn // CUTS
        half = own // 2
        up, dn, op = (y + 1) % YN, (y + YN - 1) % YN, (y + 2) % YN
        lo, hi = pl.ds(0, half), pl.ds(half, half)
        for copy in halo:
            copy.wait_recv()
        cross = rows_f32[1 : total + 1, :]
        ends = lax.broadcasted_iota(jnp.int32, (total, depth), 0) == total - 1
        cross = jnp.where(ends & (me == devices - 1), 0.0, cross).astype(jnp.bfloat16)
        a_copy, opposite, lone, shared = [], [], [], []
        for n in range(CUTS):
            for i in range(zs):
                part = weight[n * zs + i].reshape(width // zn, depth)
                product = lax.dot_general(
                    cross, part, (((1,), (1,)), ((), ())), preferred_element_type=jnp.float32
                )
                at = n * cut + i * (width // zn)
                sums[:, :, at : at + width // zn] = product.reshape(2 * YN, own, width // zn)
            cols = slice(n * cut, (n + 1) * cut)
            for other in range(YN):
                a_out[n, other] = sums[other * 2 + 1 - core, :, cols].astype(jnp.bfloat16)
            a_copy.append(
                remote(a_out.at[n], a_in.at[n], a_send.at[n], a_recv.at[n], (me, partner))
            )

        def send(src, dst, n, at, peer):
            return remote(src, dst, b_send.at[n, at], b_recv.at[n, at], (me, peer))

        def chip_sum(n):
            cols = slice(n * cut, (n + 1) * cut)
            a_copy[n].wait_recv()
            for other in range(YN):
                sums[other * 2 + core, :, cols] += a_in[n, other].astype(jnp.float32)
            far_out[n] = sums[op * 2 + core, :, cols].astype(jnp.bfloat16)
            opposite.append(
                (
                    send(far_out.at[n, lo], far_in.at[n, lo], n, 0, y_up),
                    send(far_out.at[n, hi], far_in.at[n, hi], n, 1, y_dn),
                )
            )
            near_out[n, 0, half:, :] = sums[up * 2 + core, half:, cols].astype(jnp.bfloat16)
            near_out[n, 1, :half, :] = sums[dn * 2 + core, :half, cols].astype(jnp.bfloat16)
            lone.append(
                (
                    send(near_out.at[n, 0, hi], near_in.at[n, 0, hi], n, 2, y_up),
                    send(near_out.at[n, 1, lo], near_in.at[n, 1, lo], n, 3, y_dn),
                )
            )

        def pass_on(n):
            cols = slice(n * cut, (n + 1) * cut)
            for copy in opposite[n]:
                copy.wait_recv()
            mine = sums[up * 2 + core, :half, cols] + far_in[n, :half, :].astype(jnp.float32)
            near_out[n, 0, :half, :] = mine.astype(jnp.bfloat16)
            mine = sums[dn * 2 + core, half:, cols] + far_in[n, half:, :].astype(jnp.float32)
            near_out[n, 1, half:, :] = mine.astype(jnp.bfloat16)
            shared.append(
                (
                    send(near_out.at[n, 0, lo], near_in.at[n, 0, lo], n, 4, y_up),
                    send(near_out.at[n, 1, hi], near_in.at[n, 1, hi], n, 5, y_dn),
                )
            )

        def stream(n):
            cols = slice(n * cut, (n + 1) * cut)
            for copy in lone[n] + shared[n]:
                copy.wait_recv()
            branch = sums[tens, :, cols]
            for side in range(2):
                branch += near_in[n, side].astype(jnp.float32)
            keep = drop_ref[:, cols].astype(jnp.float32) * (1.0 / keep_rate)
            value = residual_ref[:, cols].astype(jnp.float32) + keep * branch
            sums[tens, :, cols] = value
            next_ref[:, cols] = value.astype(jnp.bfloat16)
            return jnp.sum(value, axis=1, keepdims=True)

        tally = jnp.zeros((own, 1), jnp.float32)
        for n in range(CUTS + 2):
            if n < CUTS:
                chip_sum(n)
            if 1 <= n <= CUTS:
                pass_on(n - 1)
            if n >= 2:
                tally += stream(n - 2)
        centre = tally / width
        spread = jnp.zeros((own, 1), jnp.float32)
        for at in range(0, width, cut):
            off = sums[tens, :, at : at + cut] - centre
            spread += jnp.sum(off * off, axis=1, keepdims=True)
        scale = lax.rsqrt(spread / width + norm_eps)
        for at in range(0, width, cut):
            cols = slice(at, at + cut)
            normed = (sums[tens, :, cols] - centre) * scale * gain_ref[:, cols] + bias_ref[:, cols]
            normed_ref[:, cols] = normed.astype(jnp.bfloat16)

    halo = []
    live = {"c": gather_codes(), "w": gather_weight()}
    parts = {"g": gather, "k": stores, "r": reduce}
    for step in ORDER:
        for name in step:
            if name not in live:
                live[name] = parts[name[0]](int(name[1:]))
            next(live[name], None)
    for it in live.values():
        for _ in it:
            pass
    project()
    for copy in started + list(pending.values()):
        copy.wait_send()


def layer(code, q, k, v, weight, residual, drop, gain, bias):
    groups, blocks, deep, wide = q.shape
    rows = k.shape[0]
    zn = lax.axis_size("dp") // XN
    steps = zn // 2
    bf, f32 = jnp.bfloat16, jnp.float32
    own, width = residual.shape
    depth = weight.shape[1]
    cut = width // CUTS
    span = wide // GROUP
    per_group = [
        pltpu.VMEM((zn * blocks, deep, wide), bf),
        pltpu.VMEM((XN, rows, k.shape[1], GROUP * HEAD), bf),
        pltpu.VMEM((XN, rows, GROUP * HEAD, v.shape[2]), bf),
        pltpu.VMEM((zn * XN, deep, wide), bf),
        pltpu.VMEM((zn, 8, wide), f32),
        pltpu.VMEM((4, steps + 1, blocks // 2, deep, wide), bf),
        pltpu.VMEM((2, steps + 1, 8, wide), f32),
    ]
    dma = pltpu.SemaphoreType.DMA
    vmem = pl.BlockSpec(memory_space=pltpu.VMEM)
    hbm = pl.BlockSpec(memory_space=pl.ANY)
    ring = dma((groups, 4, steps))
    two = dma((groups, 4, 2))
    return pl.pallas_call(
        functools.partial(layer_kernel, zn, blocks),
        out_shape=[jax.ShapeDtypeStruct(residual.shape, bf)] * 2,
        in_specs=[vmem, vmem, hbm, hbm] + [vmem] * 5,
        out_specs=[vmem, vmem],
        scratch_shapes=per_group * groups
        + [
            pltpu.VMEM((zn, 8, HEAD), jnp.int32),
            pltpu.SMEM((zn, 8, HEAD), jnp.int32),
            pltpu.SMEM((zn, 2 * XN + 2 * blocks), jnp.int32),
            dma((2, 2)),
            dma((2, steps)),
            two,
            ring,
            dma((groups, 2)),
            dma((groups, 2, 6)),
            dma((groups, 2, 6)),
            two,
            ring,
            dma((groups, 2, 2)),
            dma((groups, 2, steps)),
            dma,
            pltpu.VMEM((zn, XN) + weight.shape, bf),
            pltpu.VMEM((4 * groups, 8, wide), f32),
            pltpu.VMEM((blocks * span + 8, depth), f32),
            pltpu.VMEM((2 * YN, own, width), f32),
            pltpu.VMEM((CUTS, YN, own, cut), bf),
            pltpu.VMEM((CUTS, YN, own, cut), bf),
            pltpu.VMEM((CUTS, own, cut), bf),
            pltpu.VMEM((CUTS, own, cut), bf),
            pltpu.VMEM((CUTS, 2, own, cut), bf),
            pltpu.VMEM((CUTS, 2, own, cut), bf),
            dma((2, 2)),
            dma((2, steps)),
            dma((6,)),
            dma((6,)),
            dma((groups,)),
            dma((groups,)),
            dma((CUTS,)),
            dma((CUTS,)),
            dma((CUTS, 6)),
            dma((CUTS, 6)),
        ],
        compiler_params=pltpu.CompilerParams(
            collective_id=0, has_side_effects=True, vmem_limit_bytes=56 * 1024 * 1024
        ),
        cost_estimate=pl.CostEstimate(
            flops=2_200_000_000, bytes_accessed=6_000_000, transcendentals=2_200_000
        ),
    )(code, q, k, v, weight, residual, drop, gain, bias)


def local(
    queries,
    neighbour_keys,
    neighbour_values,
    residual,
    out_weight,
    drop_mask,
    norm_gain,
    norm_bias,
    neighbour_owner,
    neighbour_slot,
):
    row_width = queries.shape[1]
    blocks = neighbour_owner.shape[0]
    span = queries.shape[0] // blocks
    groups = row_width // (GROUP * HEAD)
    code = (neighbour_owner * neighbour_keys.shape[0] + neighbour_slot).reshape(1, -1)
    code = jnp.pad(code, ((0, 7), (0, HEAD - code.shape[1])))
    carried = shifted(queries[-1:], "dp", 1)
    asked = jnp.concatenate([carried, queries[:-1]], axis=0)
    asked = asked.reshape(blocks, span, groups, GROUP, HEAD).transpose(2, 0, 4, 3, 1)
    asked = asked.reshape(groups, blocks, HEAD, GROUP * span)
    values = neighbour_values.transpose(0, 2, 1)
    return tuple(
        layer(
            code,
            asked,
            neighbour_keys,
            values,
            out_weight.T,
            residual,
            drop_mask,
            norm_gain.reshape(1, -1),
            norm_bias.reshape(1, -1),
        )
    )


def solution(mesh):
    placed = (
        P("dp", "tensor"),
        P("dp", None, "tensor"),
        P("dp", None, "tensor"),
        P(("dp", "tensor"), None),
        P("tensor", "dp"),
        P(("dp", "tensor"), None),
        P(),
        P(),
        P("dp", None),
        P("dp", None),
    )
    return jax.shard_map(
        local,
        mesh=mesh,
        in_specs=placed,
        out_specs=(P(("dp", "tensor"), None), P(("dp", "tensor"), None)),
        check_vma=False,
    )
```

```python
import functools

import jax
import jax.numpy as jnp
from jax import lax
from jax.experimental import pallas as pl
from jax.experimental.pallas import tpu as pltpu
from jax.sharding import PartitionSpec as P

HEAD = 128
XN = 4
GROUP = 2
NONE = -1e30

keep_rate = 0.9
norm_eps = 1e-05
MESH = pl.DeviceIdType.MESH


ORDER = (
    [("k0", "c", "g0", "g1")]
    + [("c", "g0", "g1")] * 3
    + [("c", "g0", "g1", "k0", "k1")]
    + [("w", "c", "g0", "g1")] * 3
    + [("w", "c", "c", "g0", "g1"), ("k0",)]
    + [("w", "r0")] * 3
    + [("k1", "w", "r0"), ("k1", "w", "r0", "r1"), ("w", "r0", "r1")]
    + [("r0", "r1")] * 3
    + [("w", "r1")]
    + [("r1",)] * 3
    + [("w",), ("r1",)]
)
YN = 4
CUTS = 4


def layer_kernel(
    zn,
    blocks,
    code_ref,
    q_ref,
    k_ref,
    v_ref,
    w_ref,
    residual_ref,
    drop_ref,
    gain_ref,
    bias_ref,
    next_ref,
    normed_ref,
    *scratch,
):
    total = q_ref.shape[0]
    span = total // blocks
    groups = q_ref.shape[1] // (GROUP * HEAD)
    wide = GROUP * HEAD
    rows = k_ref.shape[0]
    me = lax.axis_index("dp")
    tens = lax.axis_index("tensor")
    z, x = me // XN, me % XN
    z_up = ((z + 1) % zn) * XN + x
    z_dn = ((z + zn - 1) % zn) * XN + x
    x_up = z * XN + (x + 1) % XN
    x_dn = z * XN + (x + XN - 1) % XN
    devices = zn * XN
    d_next = (me + 1) % devices
    d_prev = (me + devices - 1) % devices
    y, core = tens // 2, tens % 2
    y_up = ((y + 1) % YN) * 2 + core
    y_dn = ((y + YN - 1) % YN) * 2 + core
    partner = y * 2 + 1 - core
    per_g = 7
    bufs = [scratch[g * per_g : (g + 1) * per_g] for g in range(groups)]
    (
        codes,
        table,
        slots,
        code_send,
        code_recv,
        ag_send,
        ag_recv,
        kv_own,
        kv_send,
        kv_recv,
        rd_send,
        rd_recv,
        rs_send,
        rs_recv,
        table_sem,
        weight,
        own_stat,
        rows_f32,
        sums,
        a_out,
        a_in,
        far_out,
        far_in,
        near_out,
        near_in,
        w_send,
        w_recv,
        wx_send,
        wx_recv,
        h_send,
        h_recv,
        a_send,
        a_recv,
        b_send,
        b_recv,
        q_f32,
        v_here,
        q_send,
        q_recv,
        v_sem,
    ) = scratch[groups * per_g :]
    far, near = zn // 2, zn // 2 - 1
    hb = blocks // 2
    chains = [
        (way, half, far if (half == 0) == (way > 0) else near)
        for half in range(2)
        for way in (1, -1)
    ]
    started, pending = [], {}

    barrier = pltpu.get_barrier_semaphore()
    for peer in (z_up, z_dn, x_up, x_dn, d_next, d_prev):
        pl.semaphore_signal(barrier, inc=1, device_id=(peer, tens), device_id_type=MESH)
    for peer in (y_up, y_dn, partner):
        pl.semaphore_signal(barrier, inc=1, device_id=(me, peer), device_id_type=MESH)
    v_copies = []
    for g in range(groups):
        copy = pltpu.make_async_copy(
            v_ref.at[:, :, pl.ds(g * wide, wide)], v_here.at[g], v_sem.at[g]
        )
        copy.start()
        v_copies.append(copy)
    q_f32[8:, :] = q_ref[...].astype(jnp.float32)
    pl.semaphore_wait(barrier, 9)

    def copy_to(src, dst, send, recv, peer):
        return pltpu.make_async_remote_copy(
            src_ref=src,
            dst_ref=dst,
            send_sem=send,
            recv_sem=recv,
            device_id=peer if isinstance(peer, tuple) else (peer, tens),
            device_id_type=MESH,
        )

    def remote(src, dst, send, recv, peer, key=None):
        copy = copy_to(src, dst, send, recv, peer)
        if key in pending:
            pending.pop(key).wait_send()
        copy.start()
        if key is None:
            started.append(copy)
        else:
            pending[key] = copy
        return copy

    def stores(g):
        hb = rows // 2
        lo, hi = pl.ds(0, hb), pl.ds(hb, hb)
        cols = pl.ds(g * wide, wide)
        keys, values = bufs[g][1:3]
        routes = ((lo, 3, x_up, 0), (hi, 1, x_dn, 1), (hi, 3, x_up, 2), (lo, 1, x_dn, 3))
        copies = {}

        def send(n, at, src, dst, peer):
            copies[n, at] = remote(src, dst, kv_send.at[g, n, at], kv_recv.at[g, n, at], peer)

        own = pltpu.make_async_copy(k_ref.at[:, :, cols], keys.at[0], kv_own.at[g])
        own.start()
        for part, place, peer, at in routes:
            send(0, at, k_ref.at[part, :, cols], keys.at[place, part], peer)
        v_copies[g].wait()

        @pl.loop(0, rows)
        def _(n):
            for h in range(GROUP):
                here = slice(h * HEAD, (h + 1) * HEAD)
                values[0, n, here, :] = jnp.transpose(v_here[g, n, :, here])

        for part, place, peer, at in routes:
            send(1, at, values.at[0, part], values.at[place, part], peer)
        yield
        for part, place, peer, at in ((lo, 3, x_up, 0), (hi, 1, x_dn, 1)):
            for n, buf in enumerate((keys, values)):
                copies[n, at].wait_recv()
                send(n, at + 4, buf.at[place, part], buf.at[2, part], peer)
        yield
        own.wait()
        for n in range(2):
            for at in range(2, 6):
                copies[n, at].wait_recv()
        yield

    def gather_codes():
        codes[z] = code_ref[...]
        for s in range(far + 1):
            for c, (way, steps) in enumerate(((1, far), (-1, near))):
                if s > steps:
                    continue
                here = codes.at[(z - way * s + zn) % zn]
                peer = z_up if way > 0 else z_dn
                if s > 0:
                    copy_to(here, here, code_send.at[c, 0], code_recv.at[c, s - 1], peer).wait_recv()
                if s < steps:
                    src = code_ref if s == 0 else here
                    remote(src, here, code_send.at[c, s % 2], code_recv.at[c, s], peer, ("c", c, s % 2))
            yield
        copy = pltpu.make_async_copy(codes, table, table_sem)
        copy.start()
        copy.wait()

        @pl.loop(0, zn)
        def _(z0):
            asks = [table[z0, 0, k] for k in range(2 * blocks)]
            for r in range(XN):
                first = (z * XN + (x + r) % XN) * rows
                block, at = jnp.int32(0), jnp.int32(0)
                for k, ask in enumerate(asks):
                    hit = (ask >= first) & (ask < first + rows)
                    block = jnp.where(hit, k // 2, block)
                    at = jnp.where(hit, ask - first, at)
                slots[z0, r] = z0 * blocks + block
                slots[z0, XN + r] = at
            for k, ask in enumerate(asks):
                holder = ask // rows
                there = holder // XN == z
                slots[z0, 2 * XN + k] = jnp.where(there, (holder - x + XN) % XN, XN)

        yield

    def own_block(g, b):
        if b == 0 and q_wait:
            q_wait.pop().wait_recv()
        top = 8 + b * span - 1
        at = g * wide
        parts = [
            q_f32[top : top + span, at + h * HEAD : at + (h + 1) * HEAD] for h in range(GROUP)
        ]
        turned = jnp.transpose(jnp.concatenate(parts, axis=0))
        if b == 0:
            row = lax.broadcasted_iota(jnp.int32, turned.shape, 1) % span
            turned = jnp.where((row == 0) & (me == 0), 0.0, turned)
        bufs[g][0][z * blocks + b] = turned.astype(jnp.bfloat16)

    q_wait = [
        remote(
            q_f32.at[pl.ds(total, 8)], q_f32.at[pl.ds(0, 8)], q_send, q_recv, d_next
        )
    ]

    def gather(g):
        col = bufs[g][0]
        for s in range(far + 1):
            for c, (way, half, steps) in enumerate(chains[::-1] if s == 0 else chains):
                c = len(chains) - 1 - c if s == 0 else c
                if s > steps:
                    continue
                at = ((z - way * s + zn) % zn) * blocks + half * hb
                here = col.at[pl.ds(at, hb)]
                peer = z_up if way > 0 else z_dn
                if s == 0 and c % 2 == 1:
                    for b in range(half * hb, (half + 1) * hb):
                        own_block(g, b)
                if s > 0:
                    copy_to(
                        here, here, ag_send.at[g, c, 0], ag_recv.at[g, c, s - 1], peer
                    ).wait_recv()
                if s < steps:
                    remote(
                        here,
                        here,
                        ag_send.at[g, c, s % 2],
                        ag_recv.at[g, c, s],
                        peer,
                        ("g", g, c, s % 2),
                    )
            yield

    left = lax.broadcasted_iota(jnp.int32, (HEAD, GROUP * span), 1) < span
    left_bf = left.astype(jnp.float32).astype(jnp.bfloat16)
    right_bf = (1.0 - left.astype(jnp.float32)).astype(jnp.bfloat16)

    def attend(g, z0):
        col, keys, values, res, stat = bufs[g][:5]
        scale = HEAD ** (-0.5)
        for pair in range(0, XN, 2):
            places = (pair, pair + 1)
            at = [slots[z0, XN + r] for r in places]
            scores = []
            for r, a in zip(places, at):
                q = col[slots[z0, r]]
                q2 = jnp.concatenate([q * left_bf, q * right_bf], axis=0)
                scores.append(jnp.dot(keys[r, a], q2, preferred_element_type=jnp.float32))
            tops = [jnp.max(v, axis=0, keepdims=True) for v in scores]
            raised = [jnp.exp((v - t) * scale) for v, t in zip(scores, tops)]
            totals = [jnp.sum(v, axis=0, keepdims=True) for v in raised]
            for r, a, e, top, total in zip(places, at, raised, tops, totals):
                eb = e.astype(jnp.bfloat16)
                p2 = jnp.concatenate([eb * left_bf, eb * right_bf], axis=0)
                v = values[r, a]
                v2 = jnp.concatenate([v[:HEAD], v[HEAD:]], axis=1)
                part = jnp.dot(v2, p2, preferred_element_type=jnp.float32)
                res[z0 * XN + r] = (part * (1.0 / total)).astype(jnp.bfloat16)
                stat[z0, r : r + 1, :] = top * scale + jnp.log(total)
        stat[z0, XN : XN + 1, :] = jnp.full((1, GROUP * span), NONE, jnp.float32)

    block_row = lax.broadcasted_iota(jnp.int32, (8, GROUP * span), 0)

    def shares(g, z0, arrived, spare):
        stat = bufs[g][4]
        for r in range(2):
            for b in range(blocks):
                place = slots[z0, 2 * XN + 2 * b + r]
                own_stat[spare + r, b : b + 1, :] = stat[z0, pl.ds(place, 1), :]
        lses = arrived + [own_stat[spare], own_stat[spare + 1]]
        top = functools.reduce(jnp.maximum, lses)
        weights = [jnp.exp(v - top) for v in lses]
        total = functools.reduce(jnp.add, weights)
        return [w / total for w in weights], top + jnp.log(total)

    def combine(g, z0, block, arrived, weights):
        res = bufs[g][3]
        vals = list(arrived)
        for r in range(2):
            place = slots[z0, 2 * XN + 2 * block + r]
            vals.append(res[z0 * XN + jnp.minimum(place, XN - 1)])
        parts = [
            v.astype(jnp.float32) * w[block : block + 1] for v, w in zip(vals, weights)
        ]
        return functools.reduce(jnp.add, parts).astype(jnp.bfloat16)

    def reduce(g):
        ring, ring_stat = bufs[g][5:7]
        for n in range(4):
            own_stat[4 * g + n] = jnp.full((8, GROUP * span), NONE, jnp.float32)
        attend(g, (z + far) % zn)
        for s in range(far):
            ways = []
            for w, way in enumerate((1, -1)):
                peer = z_up if way > 0 else z_dn
                here = ring_stat.at[w, s]
                arrived = []
                if s > 0:
                    copy_to(
                        here, here, rs_send.at[g, w, 0], rs_recv.at[g, w, s - 1], peer
                    ).wait_recv()
                    arrived = [here[...]]
                z0 = (z + way * (far - s) + zn) % zn
                weights, lse = shares(g, z0, arrived, 4 * g + 2 * w)
                if s == 0:
                    mine = (block_row < hb) == (way > 0)
                    lse = jnp.where(mine, lse, NONE)
                here[...] = lse
                remote(
                    here,
                    ring_stat.at[w, s + 1],
                    rs_send.at[g, w, s % 2],
                    rs_recv.at[g, w, s],
                    peer,
                    ("s", g, w, s % 2),
                )
                ways.append((z0, weights))
            for c, (way, half, steps) in enumerate(chains):
                i = s - (far - steps)
                if i < 0:
                    continue
                here = ring.at[c, i]
                peer = z_up if way > 0 else z_dn
                z0, weights = ways[0 if way > 0 else 1]
                if i > 0:
                    copy_to(
                        here, here, rd_send.at[g, c, 0], rd_recv.at[g, c, i - 1], peer
                    ).wait_recv()
                for b in range(hb):
                    arrived = [here[b]] if i > 0 else []
                    here[b] = combine(
                        g, z0, half * hb + b, arrived, weights[len(weights) - 2 - len(arrived) :]
                    )
                remote(
                    here,
                    ring.at[c, i + 1],
                    rd_send.at[g, c, i % 2],
                    rd_recv.at[g, c, i],
                    peer,
                    ("d", g, c, i % 2),
                )
            away = far - (s + 1)
            if away > 0:

                @pl.loop(0, 2)
                def _(n):
                    attend(g, (z + (1 - 2 * n) * away + zn) % zn)

            else:
                attend(g, z)
            yield
        arrived = []
        for w, peer in enumerate((z_up, z_dn)):
            here = ring_stat.at[w, far]
            copy_to(
                here, here, rs_send.at[g, w, 0], rs_recv.at[g, w, far - 1], peer
            ).wait_recv()
            arrived.append(here[...])
        weights, _ = shares(g, z, arrived, 4 * g)
        for c, (way, half, steps) in enumerate(chains):
            here = ring.at[c, steps]
            peer = z_up if way > 0 else z_dn
            copy_to(
                here, here, rd_send.at[g, c, 0], rd_recv.at[g, c, steps - 1], peer
            ).wait_recv()
        for b in range(blocks):
            half = b // hb
            arrived = [ring[2 * half + w, chains[2 * half + w][2], b % hb] for w in range(2)]
            rows = combine(g, z, b, arrived, weights)
            turned = jnp.transpose(rows.astype(jnp.float32))
            for h in range(GROUP):
                at = (g * GROUP + h) * HEAD
                rows_f32[b * span : (b + 1) * span, at : at + HEAD] = turned[
                    h * span : (h + 1) * span
                ]
        cols = pl.ds(g * wide, wide)
        halo.append(
            remote(
                rows_f32.at[pl.ds(0, 8), cols],
                rows_f32.at[pl.ds(blocks * span, 8), cols],
                h_send.at[g],
                h_recv.at[g],
                d_prev,
            )
        )
        yield

    def gather_weight():
        weight[z, x] = w_ref[...]
        for s in range(far + 1):
            for c, (way, steps) in enumerate(((1, far), (-1, near))):
                if s > steps:
                    continue
                here = weight.at[(z - way * s + zn) % zn, x]
                peer = z_up if way > 0 else z_dn
                if s > 0:
                    copy_to(here, here, w_send.at[c, 0], w_recv.at[c, s - 1], peer).wait_recv()
                if s < steps:
                    src = w_ref if s == 0 else here
                    remote(src, here, w_send.at[c, s % 2], w_recv.at[c, s], peer, ("w", c, s % 2))
            yield
        lo, hi = pl.ds(0, zn // 2), pl.ds(zn // 2, zn // 2)

        def send(part, column, peer, at):
            here = weight.at[part, column]
            return remote(here, here, wx_send.at[at], wx_recv.at[at], peer)

        first = [send(lo, x, x_up, 0), send(hi, x, x_dn, 1)]
        later = [send(hi, x, x_up, 2), send(lo, x, x_dn, 3)]
        yield
        first[0].wait_recv()
        later.append(send(lo, (x + XN - 1) % XN, x_up, 4))
        first[1].wait_recv()
        later.append(send(hi, (x + 1) % XN, x_dn, 5))
        yield
        for copy in later:
            copy.wait_recv()
        yield

    def project():
        width = next_ref.shape[1]
        depth = rows_f32.shape[1]
        own = total // (2 * YN)
        cut = width // CUTS
        zs = zn // CUTS
        half = own // 2
        up, dn, op = (y + 1) % YN, (y + YN - 1) % YN, (y + 2) % YN
        lo, hi = pl.ds(0, half), pl.ds(half, half)
        for copy in halo:
            copy.wait_recv()
        cross = rows_f32[1 : total + 1, :]
        ends = lax.broadcasted_iota(jnp.int32, (total, depth), 0) == total - 1
        cross = jnp.where(ends & (me == devices - 1), 0.0, cross).astype(jnp.bfloat16)
        a_copy, opposite, lone, shared = [], [], [], []
        for n in range(CUTS):
            for i in range(zs):
                part = weight[n * zs + i].reshape(width // zn, depth)
                product = lax.dot_general(
                    cross, part, (((1,), (1,)), ((), ())), preferred_element_type=jnp.float32
                )
                at = n * cut + i * (width // zn)
                sums[:, :, at : at + width // zn] = product.reshape(2 * YN, own, width // zn)
            cols = slice(n * cut, (n + 1) * cut)
            for other in range(YN):
                a_out[n, other] = sums[other * 2 + 1 - core, :, cols].astype(jnp.bfloat16)
            a_copy.append(
                remote(a_out.at[n], a_in.at[n], a_send.at[n], a_recv.at[n], (me, partner))
            )

        def send(src, dst, n, at, peer):
            return remote(src, dst, b_send.at[n, at], b_recv.at[n, at], (me, peer))

        def chip_sum(n):
            cols = slice(n * cut, (n + 1) * cut)
            a_copy[n].wait_recv()
            for other in range(YN):
                sums[other * 2 + core, :, cols] += a_in[n, other].astype(jnp.float32)
            far_out[n] = sums[op * 2 + core, :, cols].astype(jnp.bfloat16)
            opposite.append(
                (
                    send(far_out.at[n, lo], far_in.at[n, lo], n, 0, y_up),
                    send(far_out.at[n, hi], far_in.at[n, hi], n, 1, y_dn),
                )
            )
            near_out[n, 0, half:, :] = sums[up * 2 + core, half:, cols].astype(jnp.bfloat16)
            near_out[n, 1, :half, :] = sums[dn * 2 + core, :half, cols].astype(jnp.bfloat16)
            lone.append(
                (
                    send(near_out.at[n, 0, hi], near_in.at[n, 0, hi], n, 2, y_up),
                    send(near_out.at[n, 1, lo], near_in.at[n, 1, lo], n, 3, y_dn),
                )
            )

        def pass_on(n):
            cols = slice(n * cut, (n + 1) * cut)
            for copy in opposite[n]:
                copy.wait_recv()
            mine = sums[up * 2 + core, :half, cols] + far_in[n, :half, :].astype(jnp.float32)
            near_out[n, 0, :half, :] = mine.astype(jnp.bfloat16)
            mine = sums[dn * 2 + core, half:, cols] + far_in[n, half:, :].astype(jnp.float32)
            near_out[n, 1, half:, :] = mine.astype(jnp.bfloat16)
            shared.append(
                (
                    send(near_out.at[n, 0, lo], near_in.at[n, 0, lo], n, 4, y_up),
                    send(near_out.at[n, 1, hi], near_in.at[n, 1, hi], n, 5, y_dn),
                )
            )

        def stream(n):
            cols = slice(n * cut, (n + 1) * cut)
            for copy in lone[n] + shared[n]:
                copy.wait_recv()
            branch = sums[tens, :, cols]
            for side in range(2):
                branch += near_in[n, side].astype(jnp.float32)
            keep = drop_ref[:, cols].astype(jnp.float32) * (1.0 / keep_rate)
            value = residual_ref[:, cols].astype(jnp.float32) + keep * branch
            sums[tens, :, cols] = value
            next_ref[:, cols] = value.astype(jnp.bfloat16)
            return jnp.sum(value, axis=1, keepdims=True)

        tally = jnp.zeros((own, 1), jnp.float32)
        for n in range(CUTS + 2):
            if n < CUTS:
                chip_sum(n)
            if 1 <= n <= CUTS:
                pass_on(n - 1)
            if n >= 2:
                tally += stream(n - 2)
        centre = tally / width
        spread = jnp.zeros((own, 1), jnp.float32)
        for at in range(0, width, cut):
            off = sums[tens, :, at : at + cut] - centre
            spread += jnp.sum(off * off, axis=1, keepdims=True)
        scale = lax.rsqrt(spread / width + norm_eps)
        for at in range(0, width, cut):
            cols = slice(at, at + cut)
            normed = (sums[tens, :, cols] - centre) * scale * gain_ref[:, cols] + bias_ref[:, cols]
            normed_ref[:, cols] = normed.astype(jnp.bfloat16)

    halo = []
    live = {"c": gather_codes(), "w": gather_weight()}
    parts = {"g": gather, "k": stores, "r": reduce}
    for step in ORDER:
        for name in step:
            if name not in live:
                live[name] = parts[name[0]](int(name[1:]))
            next(live[name], None)
    for it in live.values():
        for _ in it:
            pass
    project()
    for copy in started + list(pending.values()):
        copy.wait_send()


def layer(blocks, code, q, k, v, weight, residual, drop, gain, bias):
    total, depth = q.shape
    groups = depth // (GROUP * HEAD)
    span = total // blocks
    deep, wide = HEAD, GROUP * span
    rows = k.shape[0]
    zn = lax.axis_size("dp") // XN
    steps = zn // 2
    bf, f32 = jnp.bfloat16, jnp.float32
    own, width = residual.shape
    cut = width // CUTS
    per_group = [
        pltpu.VMEM((zn * blocks, deep, wide), bf),
        pltpu.VMEM((XN, rows, k.shape[1], GROUP * HEAD), bf),
        pltpu.VMEM((XN, rows, GROUP * HEAD, v.shape[1]), bf),
        pltpu.VMEM((zn * XN, deep, wide), bf),
        pltpu.VMEM((zn, 8, wide), f32),
        pltpu.VMEM((4, steps + 1, blocks // 2, deep, wide), bf),
        pltpu.VMEM((2, steps + 1, 8, wide), f32),
    ]
    dma = pltpu.SemaphoreType.DMA
    vmem = pl.BlockSpec(memory_space=pltpu.VMEM)
    hbm = pl.BlockSpec(memory_space=pl.ANY)
    ring = dma((groups, 4, steps))
    two = dma((groups, 4, 2))
    return pl.pallas_call(
        functools.partial(layer_kernel, zn, blocks),
        out_shape=[jax.ShapeDtypeStruct(residual.shape, bf)] * 2,
        in_specs=[vmem, vmem, hbm, hbm] + [vmem] * 5,
        out_specs=[vmem, vmem],
        scratch_shapes=per_group * groups
        + [
            pltpu.VMEM((zn, 8, HEAD), jnp.int32),
            pltpu.SMEM((zn, 8, HEAD), jnp.int32),
            pltpu.SMEM((zn, 2 * XN + 2 * blocks), jnp.int32),
            dma((2, 2)),
            dma((2, steps)),
            two,
            ring,
            dma((groups,)),
            dma((groups, 2, 6)),
            dma((groups, 2, 6)),
            two,
            ring,
            dma((groups, 2, 2)),
            dma((groups, 2, steps)),
            dma,
            pltpu.VMEM((zn, XN) + weight.shape, bf),
            pltpu.VMEM((4 * groups, 8, wide), f32),
            pltpu.VMEM((blocks * span + 8, depth), f32),
            pltpu.VMEM((2 * YN, own, width), f32),
            pltpu.VMEM((CUTS, YN, own, cut), bf),
            pltpu.VMEM((CUTS, YN, own, cut), bf),
            pltpu.VMEM((CUTS, own, cut), bf),
            pltpu.VMEM((CUTS, own, cut), bf),
            pltpu.VMEM((CUTS, 2, own, cut), bf),
            pltpu.VMEM((CUTS, 2, own, cut), bf),
            dma((2, 2)),
            dma((2, steps)),
            dma((6,)),
            dma((6,)),
            dma((groups,)),
            dma((groups,)),
            dma((CUTS,)),
            dma((CUTS,)),
            dma((CUTS, 6)),
            dma((CUTS, 6)),
            pltpu.VMEM((8 + total, depth), f32),
            pltpu.VMEM((groups, rows, v.shape[1], GROUP * HEAD), bf),
            dma,
            dma,
            dma((groups,)),
        ],
        compiler_params=pltpu.CompilerParams(
            collective_id=0, has_side_effects=True, vmem_limit_bytes=56 * 1024 * 1024
        ),
        cost_estimate=pl.CostEstimate(
            flops=2_200_000_000, bytes_accessed=6_000_000, transcendentals=2_200_000
        ),
    )(code, q, k, v, weight, residual, drop, gain, bias)


def local(
    queries,
    neighbour_keys,
    neighbour_values,
    residual,
    out_weight,
    drop_mask,
    norm_gain,
    norm_bias,
    neighbour_owner,
    neighbour_slot,
):
    blocks = neighbour_owner.shape[0]
    code = (neighbour_owner * neighbour_keys.shape[0] + neighbour_slot).reshape(1, -1)
    code = jnp.pad(code, ((0, 7), (0, HEAD - code.shape[1])))
    return tuple(
        layer(
            blocks,
            code,
            queries,
            neighbour_keys,
            neighbour_values,
            out_weight.T,
            residual,
            drop_mask,
            norm_gain.reshape(1, -1),
            norm_bias.reshape(1, -1),
        )
    )


def solution(mesh):
    placed = (
        P("dp", "tensor"),
        P("dp", None, "tensor"),
        P("dp", None, "tensor"),
        P(("dp", "tensor"), None),
        P("tensor", "dp"),
        P(("dp", "tensor"), None),
        P(),
        P(),
        P("dp", None),
        P("dp", None),
    )
    return jax.shard_map(
        local,
        mesh=mesh,
        in_specs=placed,
        out_specs=(P(("dp", "tensor"), None), P(("dp", "tensor"), None)),
        check_vma=False,
    )
```

```python
import functools

import jax
import jax.numpy as jnp
from jax import lax
from jax.experimental import pallas as pl
from jax.experimental.pallas import tpu as pltpu
from jax.sharding import PartitionSpec as P

HEAD = 128
XN = 4
GROUP = 2
NONE = -1e30

keep_rate = 0.9
norm_eps = 1e-05
MESH = pl.DeviceIdType.MESH


ORDER = (
    [("k0", "c", "g0", "g1")]
    + [("c", "g0", "g1")] * 3
    + [("c", "g0", "g1", "k0", "k1")]
    + [("w", "c", "g0", "g1")] * 3
    + [("w", "c", "c", "g0", "g1"), ("k0",)]
    + [("w", "r0")] * 3
    + [("k1", "w", "r0"), ("k1", "w", "r0", "r1"), ("w", "r0", "r1")]
    + [("r0", "r1")] * 3
    + [("w", "r1")]
    + [("r1",)] * 3
    + [("w",), ("r1",)]
)
YN = 4
CUTS = 2


def layer_kernel(
    zn,
    blocks,
    owner_ref,
    slot_ref,
    q_ref,
    k_ref,
    v_ref,
    w_ref,
    residual_hbm,
    drop_hbm,
    gain_ref,
    bias_ref,
    next_ref,
    normed_ref,
    *scratch,
):
    total = q_ref.shape[0]
    span = total // blocks
    groups = q_ref.shape[1] // (GROUP * HEAD)
    wide = GROUP * HEAD
    rows = k_ref.shape[0]
    me = lax.axis_index("dp")
    tens = lax.axis_index("tensor")
    z, x = me // XN, me % XN
    z_up = ((z + 1) % zn) * XN + x
    z_dn = ((z + zn - 1) % zn) * XN + x
    x_up = z * XN + (x + 1) % XN
    x_dn = z * XN + (x + XN - 1) % XN
    devices = zn * XN
    d_next = (me + 1) % devices
    d_prev = (me + devices - 1) % devices
    y, core = tens // 2, tens % 2
    y_up = ((y + 1) % YN) * 2 + core
    y_dn = ((y + YN - 1) % YN) * 2 + core
    partner = y * 2 + 1 - core
    per_g = 7
    bufs = [scratch[g * per_g : (g + 1) * per_g] for g in range(groups)]
    (
        codes,
        table,
        slots,
        code_send,
        code_recv,
        ag_send,
        ag_recv,
        kv_own,
        kv_send,
        kv_recv,
        rd_send,
        rd_recv,
        rs_send,
        rs_recv,
        table_sem,
        weight,
        own_stat,
        rows_f32,
        sums,
        a_out,
        a_in,
        far_out,
        far_in,
        near_out,
        near_in,
        w_send,
        w_recv,
        wx_send,
        wx_recv,
        h_send,
        h_recv,
        a_send,
        a_recv,
        b_send,
        b_recv,
        q_f32,
        v_here,
        q_send,
        q_recv,
        v_sem,
        residual_ref,
        drop_ref,
        in_sem,
    ) = scratch[groups * per_g :]
    far, near = zn // 2, zn // 2 - 1
    hb = blocks // 2
    chains = [
        (way, half, far if (half == 0) == (way > 0) else near)
        for half in range(2)
        for way in (1, -1)
    ]
    started, pending = [], {}

    barrier = pltpu.get_barrier_semaphore()
    for peer in (z_up, z_dn, x_up, x_dn, d_next, d_prev):
        pl.semaphore_signal(barrier, inc=1, device_id=(peer, tens), device_id_type=MESH)
    for peer in (y_up, y_dn, partner):
        pl.semaphore_signal(barrier, inc=1, device_id=(me, peer), device_id_type=MESH)
    v_copies = []
    for g in range(groups):
        copy = pltpu.make_async_copy(
            v_ref.at[:, :, pl.ds(g * wide, wide)], v_here.at[g], v_sem.at[g]
        )
        copy.start()
        v_copies.append(copy)
    late = [
        pltpu.make_async_copy(residual_hbm, residual_ref, in_sem.at[0]),
        pltpu.make_async_copy(drop_hbm, drop_ref, in_sem.at[1]),
    ]
    for copy in late:
        copy.start()
    q_f32[8:, :] = q_ref[...].astype(jnp.float32)
    pl.semaphore_wait(barrier, 9)

    def copy_to(src, dst, send, recv, peer):
        return pltpu.make_async_remote_copy(
            src_ref=src,
            dst_ref=dst,
            send_sem=send,
            recv_sem=recv,
            device_id=peer if isinstance(peer, tuple) else (peer, tens),
            device_id_type=MESH,
        )

    def remote(src, dst, send, recv, peer, key=None):
        copy = copy_to(src, dst, send, recv, peer)
        if key in pending:
            pending.pop(key).wait_send()
        copy.start()
        if key is None:
            started.append(copy)
        else:
            pending[key] = copy
        return copy

    def stores(g):
        hb = rows // 2
        lo, hi = pl.ds(0, hb), pl.ds(hb, hb)
        cols = pl.ds(g * wide, wide)
        keys, values = bufs[g][1:3]
        routes = ((lo, 3, x_up, 0), (hi, 1, x_dn, 1), (hi, 3, x_up, 2), (lo, 1, x_dn, 3))
        copies = {}

        def send(n, at, src, dst, peer):
            copies[n, at] = remote(src, dst, kv_send.at[g, n, at], kv_recv.at[g, n, at], peer)

        own = pltpu.make_async_copy(k_ref.at[:, :, cols], keys.at[0], kv_own.at[g])
        own.start()
        for part, place, peer, at in routes:
            send(0, at, k_ref.at[part, :, cols], keys.at[place, part], peer)
        v_copies[g].wait()

        @pl.loop(0, rows)
        def _(n):
            for h in range(GROUP):
                here = slice(h * HEAD, (h + 1) * HEAD)
                values[0, n, here, :] = jnp.transpose(v_here[g, n, :, here])

        for part, place, peer, at in routes:
            send(1, at, values.at[0, part], values.at[place, part], peer)
        yield
        for part, place, peer, at in ((lo, 3, x_up, 0), (hi, 1, x_dn, 1)):
            for n, buf in enumerate((keys, values)):
                copies[n, at].wait_recv()
                send(n, at + 4, buf.at[place, part], buf.at[2, part], peer)
        yield
        own.wait()
        for n in range(2):
            for at in range(2, 6):
                copies[n, at].wait_recv()
        yield

    def gather_codes():
        codes[z] = jnp.zeros(codes.shape[1:], jnp.int32)
        codes[z, 0:blocks, 0:2] = owner_ref[...] * rows + slot_ref[...]
        for s in range(far + 1):
            for c, (way, steps) in enumerate(((1, far), (-1, near))):
                if s > steps:
                    continue
                here = codes.at[(z - way * s + zn) % zn]
                peer = z_up if way > 0 else z_dn
                if s > 0:
                    copy_to(here, here, code_send.at[c, 0], code_recv.at[c, s - 1], peer).wait_recv()
                if s < steps:
                    remote(here, here, code_send.at[c, s % 2], code_recv.at[c, s], peer, ("c", c, s % 2))
            yield
        copy = pltpu.make_async_copy(codes, table, table_sem)
        copy.start()
        copy.wait()

        @pl.loop(0, zn)
        def _(z0):
            asks = [table[z0, k // 2, k % 2] for k in range(2 * blocks)]
            for r in range(XN):
                first = (z * XN + (x + r) % XN) * rows
                block, at = jnp.int32(0), jnp.int32(0)
                for k, ask in enumerate(asks):
                    hit = (ask >= first) & (ask < first + rows)
                    block = jnp.where(hit, k // 2, block)
                    at = jnp.where(hit, ask - first, at)
                slots[z0, r] = z0 * blocks + block
                slots[z0, XN + r] = at
            for k, ask in enumerate(asks):
                holder = ask // rows
                there = holder // XN == z
                slots[z0, 2 * XN + k] = jnp.where(there, (holder - x + XN) % XN, XN)

        yield

    def own_block(g, b):
        if b == 0 and q_wait:
            q_wait.pop().wait_recv()
        top = 8 + b * span - 1
        at = g * wide
        parts = [
            q_f32[top : top + span, at + h * HEAD : at + (h + 1) * HEAD] for h in range(GROUP)
        ]
        turned = jnp.transpose(jnp.concatenate(parts, axis=0))
        if b == 0:
            row = lax.broadcasted_iota(jnp.int32, turned.shape, 1) % span
            turned = jnp.where((row == 0) & (me == 0), 0.0, turned)
        bufs[g][0][z * blocks + b] = turned.astype(jnp.bfloat16)

    q_wait = [
        remote(
            q_f32.at[pl.ds(total, 8)], q_f32.at[pl.ds(0, 8)], q_send, q_recv, d_next
        )
    ]

    def gather(g):
        col = bufs[g][0]
        for s in range(far + 1):
            for c, (way, half, steps) in enumerate(chains[::-1] if s == 0 else chains):
                c = len(chains) - 1 - c if s == 0 else c
                if s > steps:
                    continue
                at = ((z - way * s + zn) % zn) * blocks + half * hb
                here = col.at[pl.ds(at, hb)]
                peer = z_up if way > 0 else z_dn
                if s == 0 and c % 2 == 1:
                    for b in range(half * hb, (half + 1) * hb):
                        own_block(g, b)
                if s > 0:
                    copy_to(
                        here, here, ag_send.at[g, c, 0], ag_recv.at[g, c, s - 1], peer
                    ).wait_recv()
                if s < steps:
                    remote(
                        here,
                        here,
                        ag_send.at[g, c, s % 2],
                        ag_recv.at[g, c, s],
                        peer,
                        ("g", g, c, s % 2),
                    )
            yield

    left = lax.broadcasted_iota(jnp.int32, (HEAD, GROUP * span), 1) < span
    left_bf = left.astype(jnp.float32).astype(jnp.bfloat16)
    right_bf = (1.0 - left.astype(jnp.float32)).astype(jnp.bfloat16)

    def attend(g, z0):
        col, keys, values, res, stat = bufs[g][:5]
        scale = HEAD ** (-0.5)
        for pair in range(0, XN, 2):
            places = (pair, pair + 1)
            at = [slots[z0, XN + r] for r in places]
            scores = []
            for r, a in zip(places, at):
                q = col[slots[z0, r]]
                q2 = jnp.concatenate([q * left_bf, q * right_bf], axis=0)
                scores.append(jnp.dot(keys[r, a], q2, preferred_element_type=jnp.float32))
            tops = [jnp.max(v, axis=0, keepdims=True) for v in scores]
            raised = [jnp.exp((v - t) * scale) for v, t in zip(scores, tops)]
            totals = [jnp.sum(v, axis=0, keepdims=True) for v in raised]
            for r, a, e, top, total in zip(places, at, raised, tops, totals):
                eb = e.astype(jnp.bfloat16)
                p2 = jnp.concatenate([eb * left_bf, eb * right_bf], axis=0)
                v = values[r, a]
                v2 = jnp.concatenate([v[:HEAD], v[HEAD:]], axis=1)
                part = jnp.dot(v2, p2, preferred_element_type=jnp.float32)
                res[z0 * XN + r] = (part * (1.0 / total)).astype(jnp.bfloat16)
                stat[z0, r : r + 1, :] = top * scale + jnp.log(total)
        stat[z0, XN : XN + 1, :] = jnp.full((1, GROUP * span), NONE, jnp.float32)

    block_row = lax.broadcasted_iota(jnp.int32, (blocks, GROUP * span), 0)

    def shares(g, z0, arrived, spare):
        stat = bufs[g][4]
        for r in range(2):
            for b in range(blocks):
                place = slots[z0, 2 * XN + 2 * b + r]
                own_stat[spare + r, b : b + 1, :] = stat[z0, pl.ds(place, 1), :]
        lses = arrived + [own_stat[spare + r, 0:blocks, :] for r in range(2)]
        top = functools.reduce(jnp.maximum, lses)
        weights = [jnp.exp(v - top) for v in lses]
        total = functools.reduce(jnp.add, weights)
        return [w / total for w in weights], top + jnp.log(total)

    def combine(g, z0, block, arrived, weights):
        res = bufs[g][3]
        vals = list(arrived)
        for r in range(2):
            place = slots[z0, 2 * XN + 2 * block + r]
            vals.append(res[z0 * XN + jnp.minimum(place, XN - 1)])
        parts = [
            v.astype(jnp.float32) * w[block : block + 1] for v, w in zip(vals, weights)
        ]
        return functools.reduce(jnp.add, parts).astype(jnp.bfloat16)

    def reduce(g):
        ring, ring_stat = bufs[g][5:7]
        attend(g, (z + far) % zn)
        for s in range(far):
            ways = []
            for w, way in enumerate((1, -1)):
                peer = z_up if way > 0 else z_dn
                here = ring_stat.at[w, s, pl.ds(0, blocks)]
                arrived = []
                if s > 0:
                    copy_to(
                        here, here, rs_send.at[g, w, 0], rs_recv.at[g, w, s - 1], peer
                    ).wait_recv()
                    arrived = [here[...]]
                z0 = (z + way * (far - s) + zn) % zn
                weights, lse = shares(g, z0, arrived, 4 * g + 2 * w)
                if s == 0:
                    mine = (block_row < hb) == (way > 0)
                    lse = jnp.where(mine, lse, NONE)
                here[...] = lse
                remote(
                    here,
                    ring_stat.at[w, s + 1, pl.ds(0, blocks)],
                    rs_send.at[g, w, s % 2],
                    rs_recv.at[g, w, s],
                    peer,
                    ("s", g, w, s % 2),
                )
                ways.append((z0, weights))
            for c, (way, half, steps) in enumerate(chains):
                i = s - (far - steps)
                if i < 0:
                    continue
                here = ring.at[c, i]
                peer = z_up if way > 0 else z_dn
                z0, weights = ways[0 if way > 0 else 1]
                if i > 0:
                    copy_to(
                        here, here, rd_send.at[g, c, 0], rd_recv.at[g, c, i - 1], peer
                    ).wait_recv()
                for b in range(hb):
                    arrived = [here[b]] if i > 0 else []
                    here[b] = combine(
                        g, z0, half * hb + b, arrived, weights[len(weights) - 2 - len(arrived) :]
                    )
                remote(
                    here,
                    ring.at[c, i + 1],
                    rd_send.at[g, c, i % 2],
                    rd_recv.at[g, c, i],
                    peer,
                    ("d", g, c, i % 2),
                )
            away = far - (s + 1)
            if away > 0:

                @pl.loop(0, 2)
                def _(n):
                    attend(g, (z + (1 - 2 * n) * away + zn) % zn)

            else:
                attend(g, z)
            yield
        arrived = []
        for w, peer in enumerate((z_up, z_dn)):
            here = ring_stat.at[w, far, pl.ds(0, blocks)]
            copy_to(
                here, here, rs_send.at[g, w, 0], rs_recv.at[g, w, far - 1], peer
            ).wait_recv()
            arrived.append(here[...])
        weights, _ = shares(g, z, arrived, 4 * g)
        for c, (way, half, steps) in enumerate(chains):
            here = ring.at[c, steps]
            peer = z_up if way > 0 else z_dn
            copy_to(
                here, here, rd_send.at[g, c, 0], rd_recv.at[g, c, steps - 1], peer
            ).wait_recv()
        for b in range(blocks):
            half = b // hb
            arrived = [ring[2 * half + w, chains[2 * half + w][2], b % hb] for w in range(2)]
            rows = combine(g, z, b, arrived, weights)
            turned = jnp.transpose(rows.astype(jnp.float32))
            for h in range(GROUP):
                at = (g * GROUP + h) * HEAD
                rows_f32[b * span : (b + 1) * span, at : at + HEAD] = turned[
                    h * span : (h + 1) * span
                ]
            if b == 0:
                cols = pl.ds(g * wide, wide)
                halo.append(
                    remote(
                        rows_f32.at[pl.ds(0, 8), cols],
                        rows_f32.at[pl.ds(blocks * span, 8), cols],
                        h_send.at[g],
                        h_recv.at[g],
                        d_prev,
                    )
                )
        yield

    def gather_weight():
        weight[z, x] = w_ref[...]
        for s in range(far + 1):
            for c, (way, steps) in enumerate(((1, far), (-1, near))):
                if s > steps:
                    continue
                here = weight.at[(z - way * s + zn) % zn, x]
                peer = z_up if way > 0 else z_dn
                if s > 0:
                    copy_to(here, here, w_send.at[c, 0], w_recv.at[c, s - 1], peer).wait_recv()
                if s < steps:
                    src = w_ref if s == 0 else here
                    remote(src, here, w_send.at[c, s % 2], w_recv.at[c, s], peer, ("w", c, s % 2))
            yield
        lo, hi = pl.ds(0, zn // 2), pl.ds(zn // 2, zn // 2)

        def send(part, column, peer, at):
            here = weight.at[part, column]
            return remote(here, here, wx_send.at[at], wx_recv.at[at], peer)

        first = [send(lo, x, x_up, 0), send(hi, x, x_dn, 1)]
        later = [send(hi, x, x_up, 2), send(lo, x, x_dn, 3)]
        yield
        first[0].wait_recv()
        later.append(send(lo, (x + XN - 1) % XN, x_up, 4))
        first[1].wait_recv()
        later.append(send(hi, (x + 1) % XN, x_dn, 5))
        yield
        for copy in later:
            copy.wait_recv()
        yield

    def project():
        width = next_ref.shape[1]
        depth = rows_f32.shape[1]
        own = total // (2 * YN)
        cut = width // CUTS
        zs = zn // CUTS
        half = own // 2
        up, dn, op = (y + 1) % YN, (y + YN - 1) % YN, (y + 2) % YN
        lo, hi = pl.ds(0, half), pl.ds(half, half)
        for copy in late:
            copy.wait()
        for copy in halo:
            copy.wait_recv()
        cross = rows_f32[1 : total + 1, :]
        ends = lax.broadcasted_iota(jnp.int32, (total, depth), 0) == total - 1
        cross = jnp.where(ends & (me == devices - 1), 0.0, cross).astype(jnp.bfloat16)
        a_copy, opposite, lone, shared = [], [], [], []
        for n in range(CUTS):
            for i in range(zs):
                part = weight[n * zs + i].reshape(width // zn, depth)
                product = lax.dot_general(
                    cross, part, (((1,), (1,)), ((), ())), preferred_element_type=jnp.float32
                )
                at = n * cut + i * (width // zn)
                sums[:, :, at : at + width // zn] = product.reshape(2 * YN, own, width // zn)
            cols = slice(n * cut, (n + 1) * cut)
            for other in range(YN):
                a_out[n, other] = sums[other * 2 + 1 - core, :, cols].astype(jnp.bfloat16)
            a_copy.append(
                remote(a_out.at[n], a_in.at[n], a_send.at[n], a_recv.at[n], (me, partner))
            )

        def send(src, dst, n, at, peer):
            return remote(src, dst, b_send.at[n, at], b_recv.at[n, at], (me, peer))

        def chip_sum(n):
            cols = slice(n * cut, (n + 1) * cut)
            a_copy[n].wait_recv()
            for other in range(YN):
                sums[other * 2 + core, :, cols] += a_in[n, other].astype(jnp.float32)
            far_out[n] = sums[op * 2 + core, :, cols].astype(jnp.bfloat16)
            opposite.append(
                (
                    send(far_out.at[n, lo], far_in.at[n, lo], n, 0, y_up),
                    send(far_out.at[n, hi], far_in.at[n, hi], n, 1, y_dn),
                )
            )
            near_out[n, 0, half:, :] = sums[up * 2 + core, half:, cols].astype(jnp.bfloat16)
            near_out[n, 1, :half, :] = sums[dn * 2 + core, :half, cols].astype(jnp.bfloat16)
            lone.append(
                (
                    send(near_out.at[n, 0, hi], near_in.at[n, 0, hi], n, 2, y_up),
                    send(near_out.at[n, 1, lo], near_in.at[n, 1, lo], n, 3, y_dn),
                )
            )

        def pass_on(n):
            cols = slice(n * cut, (n + 1) * cut)
            for copy in opposite[n]:
                copy.wait_recv()
            mine = sums[up * 2 + core, :half, cols] + far_in[n, :half, :].astype(jnp.float32)
            near_out[n, 0, :half, :] = mine.astype(jnp.bfloat16)
            mine = sums[dn * 2 + core, half:, cols] + far_in[n, half:, :].astype(jnp.float32)
            near_out[n, 1, half:, :] = mine.astype(jnp.bfloat16)
            shared.append(
                (
                    send(near_out.at[n, 0, lo], near_in.at[n, 0, lo], n, 4, y_up),
                    send(near_out.at[n, 1, hi], near_in.at[n, 1, hi], n, 5, y_dn),
                )
            )

        def stream(n):
            cols = slice(n * cut, (n + 1) * cut)
            for copy in lone[n] + shared[n]:
                copy.wait_recv()
            branch = sums[tens, :, cols]
            for side in range(2):
                branch += near_in[n, side].astype(jnp.float32)
            keep = drop_ref[:, cols].astype(jnp.float32) * (1.0 / keep_rate)
            value = residual_ref[:, cols].astype(jnp.float32) + keep * branch
            sums[tens, :, cols] = value
            next_ref[:, cols] = value.astype(jnp.bfloat16)
            return jnp.sum(value, axis=1, keepdims=True)

        tally = jnp.zeros((own, 1), jnp.float32)
        for n in range(CUTS + 2):
            if n < CUTS:
                chip_sum(n)
            if 1 <= n <= CUTS:
                pass_on(n - 1)
            if n >= 2:
                tally += stream(n - 2)
        centre = tally / width
        spread = jnp.zeros((own, 1), jnp.float32)
        for at in range(0, width, cut):
            off = sums[tens, :, at : at + cut] - centre
            spread += jnp.sum(off * off, axis=1, keepdims=True)
        scale = lax.rsqrt(spread / width + norm_eps)
        for at in range(0, width, cut):
            cols = slice(at, at + cut)
            normed = (sums[tens, :, cols] - centre) * scale * gain_ref[:, cols] + bias_ref[:, cols]
            normed_ref[:, cols] = normed.astype(jnp.bfloat16)

    halo = []
    live = {"c": gather_codes(), "w": gather_weight()}
    parts = {"g": gather, "k": stores, "r": reduce}
    for step in ORDER:
        for name in step:
            if name not in live:
                live[name] = parts[name[0]](int(name[1:]))
            next(live[name], None)
    for it in live.values():
        for _ in it:
            pass
    project()
    for copy in started + list(pending.values()):
        copy.wait_send()


def layer(owner, slot, q, k, v, weight, residual, drop, gain, bias):
    total, depth = q.shape
    blocks = owner.shape[0]
    groups = depth // (GROUP * HEAD)
    span = total // blocks
    deep, wide = HEAD, GROUP * span
    rows = k.shape[0]
    zn = lax.axis_size("dp") // XN
    steps = zn // 2
    bf, f32 = jnp.bfloat16, jnp.float32
    own, width = residual.shape
    cut = width // CUTS
    per_group = [
        pltpu.VMEM((zn * blocks, deep, wide), bf),
        pltpu.VMEM((XN, rows, k.shape[1], GROUP * HEAD), bf),
        pltpu.VMEM((XN, rows, GROUP * HEAD, v.shape[1]), bf),
        pltpu.VMEM((zn * XN, deep, wide), bf),
        pltpu.VMEM((zn, 8, wide), f32),
        pltpu.VMEM((4, steps + 1, blocks // 2, deep, wide), bf),
        pltpu.VMEM((2, steps + 1, 8, wide), f32),
    ]
    dma = pltpu.SemaphoreType.DMA
    vmem = pl.BlockSpec(memory_space=pltpu.VMEM)
    hbm = pl.BlockSpec(memory_space=pl.ANY)
    ring = dma((groups, 4, steps))
    two = dma((groups, 4, 2))
    return pl.pallas_call(
        functools.partial(layer_kernel, zn, blocks),
        out_shape=[jax.ShapeDtypeStruct(residual.shape, bf)] * 2,
        in_specs=[vmem] * 3 + [hbm, hbm, vmem, hbm, hbm, vmem, vmem],
        out_specs=[vmem, vmem],
        scratch_shapes=per_group * groups
        + [
            pltpu.VMEM((zn, 8, HEAD), jnp.int32),
            pltpu.SMEM((zn, 8, HEAD), jnp.int32),
            pltpu.SMEM((zn, 2 * XN + 2 * blocks), jnp.int32),
            dma((2, 2)),
            dma((2, steps)),
            two,
            ring,
            dma((groups,)),
            dma((groups, 2, 6)),
            dma((groups, 2, 6)),
            two,
            ring,
            dma((groups, 2, 2)),
            dma((groups, 2, steps)),
            dma,
            pltpu.VMEM((zn, XN) + weight.shape, bf),
            pltpu.VMEM((4 * groups, 8, wide), f32),
            pltpu.VMEM((blocks * span + 8, depth), f32),
            pltpu.VMEM((2 * YN, own, width), f32),
            pltpu.VMEM((CUTS, YN, own, cut), bf),
            pltpu.VMEM((CUTS, YN, own, cut), bf),
            pltpu.VMEM((CUTS, own, cut), bf),
            pltpu.VMEM((CUTS, own, cut), bf),
            pltpu.VMEM((CUTS, 2, own, cut), bf),
            pltpu.VMEM((CUTS, 2, own, cut), bf),
            dma((2, 2)),
            dma((2, steps)),
            dma((6,)),
            dma((6,)),
            dma((groups,)),
            dma((groups,)),
            dma((CUTS,)),
            dma((CUTS,)),
            dma((CUTS, 6)),
            dma((CUTS, 6)),
            pltpu.VMEM((8 + total, depth), f32),
            pltpu.VMEM((groups, rows, v.shape[1], GROUP * HEAD), bf),
            dma,
            dma,
            dma((groups,)),
            pltpu.VMEM(residual.shape, residual.dtype),
            pltpu.VMEM(drop.shape, drop.dtype),
            dma((2,)),
        ],
        compiler_params=pltpu.CompilerParams(
            collective_id=0, has_side_effects=True, vmem_limit_bytes=56 * 1024 * 1024
        ),
        cost_estimate=pl.CostEstimate(
            flops=2_200_000_000, bytes_accessed=6_000_000, transcendentals=2_200_000
        ),
    )(owner, slot, q, k, v, weight, residual, drop, gain, bias)


def local(
    queries,
    neighbour_keys,
    neighbour_values,
    residual,
    out_weight,
    drop_mask,
    norm_gain,
    norm_bias,
    neighbour_owner,
    neighbour_slot,
):
    return tuple(
        layer(
            neighbour_owner,
            neighbour_slot,
            queries,
            neighbour_keys,
            neighbour_values,
            out_weight.T,
            residual,
            drop_mask,
            norm_gain.reshape(1, -1),
            norm_bias.reshape(1, -1),
        )
    )


def solution(mesh):
    placed = (
        P("dp", "tensor"),
        P("dp", None, "tensor"),
        P("dp", None, "tensor"),
        P(("dp", "tensor"), None),
        P("tensor", "dp"),
        P(("dp", "tensor"), None),
        P(),
        P(),
        P("dp", None),
        P("dp", None),
    )
    return jax.shard_map(
        local,
        mesh=mesh,
        in_specs=placed,
        out_specs=(P(("dp", "tensor"), None), P(("dp", "tensor"), None)),
        check_vma=False,
    )
```

```python
import functools

import jax
import jax.numpy as jnp
from jax import lax
from jax.experimental import pallas as pl
from jax.experimental.pallas import tpu as pltpu
from jax.sharding import PartitionSpec as P

HEAD = 128
XN = 4
GROUP = 2
NONE = -1e30

keep_rate = 0.9
norm_eps = 1e-05
MESH = pl.DeviceIdType.MESH


ORDER = (
    [("k0", "c", "g0", "g1")]
    + [("c", "g0", "g1")] * 3
    + [("c", "g0", "g1", "k0", "k1")]
    + [("c", "g0", "g1", "w")] * 3
    + [("c", "c", "g0", "g1", "w"), ("k0",)]
    + [("r0", "w")] * 3
    + [("k1", "r0", "w"), ("k1", "r0", "r1", "w"), ("r0", "r1", "w")]
    + [("r0", "r1")] * 3
    + [("r1", "w")]
    + [("r1",)] * 3
    + [("w",), ("r1",)]
)
YN = 4
CUTS = 2


def layer_kernel(
    zn,
    blocks,
    owner_ref,
    slot_ref,
    q_ref,
    k_ref,
    v_ref,
    w_ref,
    residual_hbm,
    drop_hbm,
    gain_ref,
    bias_ref,
    next_ref,
    normed_ref,
    *scratch,
):
    total = q_ref.shape[0]
    span = total // blocks
    groups = q_ref.shape[1] // (GROUP * HEAD)
    wide = GROUP * HEAD
    rows = k_ref.shape[0]
    me = lax.axis_index("dp")
    tens = lax.axis_index("tensor")
    z, x = me // XN, me % XN
    z_up = ((z + 1) % zn) * XN + x
    z_dn = ((z + zn - 1) % zn) * XN + x
    x_up = z * XN + (x + 1) % XN
    x_dn = z * XN + (x + XN - 1) % XN
    devices = zn * XN
    d_next = (me + 1) % devices
    d_prev = (me + devices - 1) % devices
    y, core = tens // 2, tens % 2
    y_up = ((y + 1) % YN) * 2 + core
    y_dn = ((y + YN - 1) % YN) * 2 + core
    partner = y * 2 + 1 - core
    per_g = 7
    bufs = [scratch[g * per_g : (g + 1) * per_g] for g in range(groups)]
    (
        codes,
        table,
        slots,
        code_send,
        code_recv,
        ag_send,
        ag_recv,
        kv_own,
        kv_send,
        kv_recv,
        rd_send,
        rd_recv,
        rs_send,
        rs_recv,
        table_sem,
        weight,
        own_stat,
        rows_f32,
        sums,
        a_out,
        a_in,
        far_out,
        far_in,
        near_out,
        near_in,
        w_send,
        w_recv,
        wx_send,
        wx_recv,
        h_send,
        h_recv,
        a_send,
        a_recv,
        b_send,
        b_recv,
        q_f32,
        v_here,
        q_send,
        q_recv,
        v_sem,
        residual_ref,
        drop_ref,
        in_sem,
    ) = scratch[groups * per_g :]
    far, near = zn // 2, zn // 2 - 1
    hb = blocks // 2
    chains = [
        (way, half, far if (half == 0) == (way > 0) else near)
        for half in range(2)
        for way in (1, -1)
    ]
    started, pending = [], {}

    barrier = pltpu.get_barrier_semaphore()
    for peer in (z_up, z_dn, x_up, x_dn, d_next, d_prev):
        pl.semaphore_signal(barrier, inc=1, device_id=(peer, tens), device_id_type=MESH)
    for peer in (y_up, y_dn, partner):
        pl.semaphore_signal(barrier, inc=1, device_id=(me, peer), device_id_type=MESH)
    v_copies = []
    for g in range(groups):
        copy = pltpu.make_async_copy(
            v_ref.at[:, :, pl.ds(g * wide, wide)], v_here.at[g], v_sem.at[g]
        )
        copy.start()
        v_copies.append(copy)
    late = [
        pltpu.make_async_copy(residual_hbm, residual_ref, in_sem.at[0]),
        pltpu.make_async_copy(drop_hbm, drop_ref, in_sem.at[1]),
    ]
    for copy in late:
        copy.start()
    q_f32[8:, :] = q_ref[...].astype(jnp.float32)
    pl.semaphore_wait(barrier, 9)

    def copy_to(src, dst, send, recv, peer):
        return pltpu.make_async_remote_copy(
            src_ref=src,
            dst_ref=dst,
            send_sem=send,
            recv_sem=recv,
            device_id=peer if isinstance(peer, tuple) else (peer, tens),
            device_id_type=MESH,
        )

    def remote(src, dst, send, recv, peer, key=None):
        copy = copy_to(src, dst, send, recv, peer)
        if key in pending:
            pending.pop(key).wait_send()
        copy.start()
        if key is None:
            started.append(copy)
        else:
            pending[key] = copy
        return copy

    def stores(g):
        hb = rows // 2
        lo, hi = pl.ds(0, hb), pl.ds(hb, hb)
        cols = pl.ds(g * wide, wide)
        keys, values = bufs[g][1:3]
        routes = ((lo, 3, x_up, 0), (hi, 1, x_dn, 1), (hi, 3, x_up, 2), (lo, 1, x_dn, 3))
        copies = {}

        def send(n, at, src, dst, peer):
            copies[n, at] = remote(src, dst, kv_send.at[g, n, at], kv_recv.at[g, n, at], peer)

        own = pltpu.make_async_copy(k_ref.at[:, :, cols], keys.at[0], kv_own.at[g])
        own.start()
        for part, place, peer, at in routes:
            send(0, at, k_ref.at[part, :, cols], keys.at[place, part], peer)
        v_copies[g].wait()

        @pl.loop(0, rows)
        def _(n):
            for h in range(GROUP):
                here = slice(h * HEAD, (h + 1) * HEAD)
                values[0, n, here, :] = jnp.transpose(v_here[g, n, :, here])

        for part, place, peer, at in routes:
            send(1, at, values.at[0, part], values.at[place, part], peer)
        yield
        for part, place, peer, at in ((lo, 3, x_up, 0), (hi, 1, x_dn, 1)):
            for n, buf in enumerate((keys, values)):
                copies[n, at].wait_recv()
                send(n, at + 4, buf.at[place, part], buf.at[2, part], peer)
        yield
        own.wait()
        for n in range(2):
            for at in range(2, 6):
                copies[n, at].wait_recv()
        yield

    def gather_codes():
        codes[z] = jnp.zeros(codes.shape[1:], jnp.int32)
        codes[z, 0:blocks, 0:2] = owner_ref[...] * rows + slot_ref[...]
        for s in range(far + 1):
            for c, (way, steps) in enumerate(((1, far), (-1, near))):
                if s > steps:
                    continue
                here = codes.at[(z - way * s + zn) % zn]
                peer = z_up if way > 0 else z_dn
                if s > 0:
                    copy_to(here, here, code_send.at[c, 0], code_recv.at[c, s - 1], peer).wait_recv()
                if s < steps:
                    remote(here, here, code_send.at[c, s % 2], code_recv.at[c, s], peer, ("c", c, s % 2))
            yield
        copy = pltpu.make_async_copy(codes, table, table_sem)
        copy.start()
        copy.wait()

        @pl.loop(0, zn)
        def _(z0):
            asks = [table[z0, k // 2, k % 2] for k in range(2 * blocks)]
            for r in range(XN):
                first = (z * XN + (x + r) % XN) * rows
                block, at = jnp.int32(0), jnp.int32(0)
                for k, ask in enumerate(asks):
                    hit = (ask >= first) & (ask < first + rows)
                    block = jnp.where(hit, k // 2, block)
                    at = jnp.where(hit, ask - first, at)
                slots[z0, r] = z0 * blocks + block
                slots[z0, XN + r] = at
            for k, ask in enumerate(asks):
                holder = ask // rows
                there = holder // XN == z
                slots[z0, 2 * XN + k] = jnp.where(there, (holder - x + XN) % XN, XN)

        yield

    def own_block(g, b):
        if b == 0 and q_wait:
            q_wait.pop().wait_recv()
        top = 8 + b * span - 1
        at = g * wide
        parts = [
            q_f32[top : top + span, at + h * HEAD : at + (h + 1) * HEAD] for h in range(GROUP)
        ]
        turned = jnp.transpose(jnp.concatenate(parts, axis=0))
        if b == 0:
            row = lax.broadcasted_iota(jnp.int32, turned.shape, 1) % span
            turned = jnp.where((row == 0) & (me == 0), 0.0, turned)
        bufs[g][0][z * blocks + b] = turned.astype(jnp.bfloat16)

    q_wait = [
        remote(
            q_f32.at[pl.ds(total, 8)], q_f32.at[pl.ds(0, 8)], q_send, q_recv, d_next
        )
    ]

    def gather(g):
        col = bufs[g][0]
        for s in range(far + 1):
            for c, (way, half, steps) in enumerate(chains[::-1] if s == 0 else chains):
                c = len(chains) - 1 - c if s == 0 else c
                if s > steps:
                    continue
                at = ((z - way * s + zn) % zn) * blocks + half * hb
                here = col.at[pl.ds(at, hb)]
                peer = z_up if way > 0 else z_dn
                if s == 0 and c % 2 == 1:
                    for b in range(half * hb, (half + 1) * hb):
                        own_block(g, b)
                if s > 0:
                    copy_to(
                        here, here, ag_send.at[g, c, 0], ag_recv.at[g, c, s - 1], peer
                    ).wait_recv()
                if s < steps:
                    remote(
                        here,
                        here,
                        ag_send.at[g, c, s % 2],
                        ag_recv.at[g, c, s],
                        peer,
                        ("g", g, c, s % 2),
                    )
            yield

    left = lax.broadcasted_iota(jnp.int32, (HEAD, GROUP * span), 1) < span
    left_bf = left.astype(jnp.float32).astype(jnp.bfloat16)
    right_bf = (1.0 - left.astype(jnp.float32)).astype(jnp.bfloat16)

    def attend(g, z0):
        col, keys, values, res, stat = bufs[g][:5]
        scale = HEAD ** (-0.5)
        for pair in range(0, XN, 2):
            places = (pair, pair + 1)
            at = [slots[z0, XN + r] for r in places]
            scores = []
            for r, a in zip(places, at):
                q = col[slots[z0, r]]
                q2 = jnp.concatenate([q * left_bf, q * right_bf], axis=0)
                scores.append(jnp.dot(keys[r, a], q2, preferred_element_type=jnp.float32))
            tops = [jnp.max(v, axis=0, keepdims=True) for v in scores]
            raised = [jnp.exp((v - t) * scale) for v, t in zip(scores, tops)]
            totals = [jnp.sum(v, axis=0, keepdims=True) for v in raised]
            for r, a, e, top, total in zip(places, at, raised, tops, totals):
                eb = e.astype(jnp.bfloat16)
                p2 = jnp.concatenate([eb * left_bf, eb * right_bf], axis=0)
                v = values[r, a]
                v2 = jnp.concatenate([v[:HEAD], v[HEAD:]], axis=1)
                part = jnp.dot(v2, p2, preferred_element_type=jnp.float32)
                res[z0 * XN + r] = (part * (1.0 / total)).astype(jnp.bfloat16)
                stat[z0, r : r + 1, :] = top * scale + jnp.log(total)
        stat[z0, XN : XN + 1, :] = jnp.full((1, GROUP * span), NONE, jnp.float32)

    block_row = lax.broadcasted_iota(jnp.int32, (blocks, GROUP * span), 0)

    def shares(g, z0, arrived, spare):
        stat = bufs[g][4]
        for r in range(2):
            for b in range(blocks):
                place = slots[z0, 2 * XN + 2 * b + r]
                own_stat[spare + r, b : b + 1, :] = stat[z0, pl.ds(place, 1), :]
        lses = arrived + [own_stat[spare + r, 0:blocks, :] for r in range(2)]
        top = functools.reduce(jnp.maximum, lses)
        weights = [jnp.exp(v - top) for v in lses]
        total = functools.reduce(jnp.add, weights)
        return [w / total for w in weights], top + jnp.log(total)

    def combine(g, z0, block, arrived, weights):
        res = bufs[g][3]
        vals = list(arrived)
        for r in range(2):
            place = slots[z0, 2 * XN + 2 * block + r]
            vals.append(res[z0 * XN + jnp.minimum(place, XN - 1)])
        parts = [
            v.astype(jnp.float32) * w[block : block + 1] for v, w in zip(vals, weights)
        ]
        return functools.reduce(jnp.add, parts).astype(jnp.bfloat16)

    def reduce(g):
        ring, ring_stat = bufs[g][5:7]
        attend(g, (z + far) % zn)
        for s in range(far):
            ways = []
            for w, way in enumerate((1, -1)):
                peer = z_up if way > 0 else z_dn
                here = ring_stat.at[w, s, pl.ds(0, blocks)]
                arrived = []
                if s > 0:
                    copy_to(
                        here, here, rs_send.at[g, w, 0], rs_recv.at[g, w, s - 1], peer
                    ).wait_recv()
                    arrived = [here[...]]
                z0 = (z + way * (far - s) + zn) % zn
                weights, lse = shares(g, z0, arrived, 4 * g + 2 * w)
                if s == 0:
                    mine = (block_row < hb) == (way > 0)
                    lse = jnp.where(mine, lse, NONE)
                here[...] = lse
                remote(
                    here,
                    ring_stat.at[w, s + 1, pl.ds(0, blocks)],
                    rs_send.at[g, w, s % 2],
                    rs_recv.at[g, w, s],
                    peer,
                    ("s", g, w, s % 2),
                )
                ways.append((z0, weights))
            for c, (way, half, steps) in enumerate(chains):
                i = s - (far - steps)
                if i < 0:
                    continue
                here = ring.at[c, i]
                peer = z_up if way > 0 else z_dn
                z0, weights = ways[0 if way > 0 else 1]
                if i > 0:
                    copy_to(
                        here, here, rd_send.at[g, c, 0], rd_recv.at[g, c, i - 1], peer
                    ).wait_recv()
                for b in range(hb):
                    arrived = [here[b]] if i > 0 else []
                    here[b] = combine(
                        g, z0, half * hb + b, arrived, weights[len(weights) - 2 - len(arrived) :]
                    )
                remote(
                    here,
                    ring.at[c, i + 1],
                    rd_send.at[g, c, i % 2],
                    rd_recv.at[g, c, i],
                    peer,
                    ("d", g, c, i % 2),
                )
            away = far - (s + 1)
            if away > 0:

                @pl.loop(0, 2)
                def _(n):
                    attend(g, (z + (1 - 2 * n) * away + zn) % zn)

            else:
                attend(g, z)
            yield
        arrived = []
        for w, peer in enumerate((z_up, z_dn)):
            here = ring_stat.at[w, far, pl.ds(0, blocks)]
            copy_to(
                here, here, rs_send.at[g, w, 0], rs_recv.at[g, w, far - 1], peer
            ).wait_recv()
            arrived.append(here[...])
        weights, _ = shares(g, z, arrived, 4 * g)
        for c, (way, half, steps) in enumerate(chains):
            here = ring.at[c, steps]
            peer = z_up if way > 0 else z_dn
            copy_to(
                here, here, rd_send.at[g, c, 0], rd_recv.at[g, c, steps - 1], peer
            ).wait_recv()
        for b in range(blocks):
            half = b // hb
            arrived = [ring[2 * half + w, chains[2 * half + w][2], b % hb] for w in range(2)]
            rows = combine(g, z, b, arrived, weights)
            turned = jnp.transpose(rows.astype(jnp.float32))
            for h in range(GROUP):
                at = (g * GROUP + h) * HEAD
                rows_f32[b * span : (b + 1) * span, at : at + HEAD] = turned[
                    h * span : (h + 1) * span
                ]
            if b == 0:
                cols = pl.ds(g * wide, wide)
                halo.append(
                    remote(
                        rows_f32.at[pl.ds(0, 8), cols],
                        rows_f32.at[pl.ds(blocks * span, 8), cols],
                        h_send.at[g],
                        h_recv.at[g],
                        d_prev,
                    )
                )
        yield

    def gather_weight():
        weight[z, x] = w_ref[...]
        for s in range(far + 1):
            for c, (way, steps) in enumerate(((1, far), (-1, near))):
                if s > steps:
                    continue
                here = weight.at[(z - way * s + zn) % zn, x]
                peer = z_up if way > 0 else z_dn
                if s > 0:
                    copy_to(here, here, w_send.at[c, 0], w_recv.at[c, s - 1], peer).wait_recv()
                if s < steps:
                    src = w_ref if s == 0 else here
                    remote(src, here, w_send.at[c, s % 2], w_recv.at[c, s], peer, ("w", c, s % 2))
            yield
        lo, hi = pl.ds(0, zn // 2), pl.ds(zn // 2, zn // 2)

        def send(part, column, peer, at):
            here = weight.at[part, column]
            return remote(here, here, wx_send.at[at], wx_recv.at[at], peer)

        first = [send(lo, x, x_up, 0), send(hi, x, x_dn, 1)]
        later = [send(hi, x, x_up, 2), send(lo, x, x_dn, 3)]
        yield
        first[0].wait_recv()
        later.append(send(lo, (x + XN - 1) % XN, x_up, 4))
        first[1].wait_recv()
        later.append(send(hi, (x + 1) % XN, x_dn, 5))
        yield
        for copy in later:
            copy.wait_recv()
        yield

    def project():
        width = next_ref.shape[1]
        depth = rows_f32.shape[1]
        own = total // (2 * YN)
        cut = width // CUTS
        zs = zn // CUTS
        half = own // 2
        up, dn, op = (y + 1) % YN, (y + YN - 1) % YN, (y + 2) % YN
        lo, hi = pl.ds(0, half), pl.ds(half, half)
        for copy in late:
            copy.wait()
        for copy in halo:
            copy.wait_recv()
        cross = rows_f32[1 : total + 1, :]
        ends = lax.broadcasted_iota(jnp.int32, (total, depth), 0) == total - 1
        cross = jnp.where(ends & (me == devices - 1), 0.0, cross).astype(jnp.bfloat16)
        a_copy, opposite, lone, shared = [], [], [], []
        for n in range(CUTS):
            for i in range(zs):
                part = weight[n * zs + i].reshape(width // zn, depth)
                product = lax.dot_general(
                    cross, part, (((1,), (1,)), ((), ())), preferred_element_type=jnp.float32
                )
                at = n * cut + i * (width // zn)
                sums[:, :, at : at + width // zn] = product.reshape(2 * YN, own, width // zn)
            cols = slice(n * cut, (n + 1) * cut)
            for other in range(YN):
                a_out[n, other] = sums[other * 2 + 1 - core, :, cols].astype(jnp.bfloat16)
            a_copy.append(
                remote(a_out.at[n], a_in.at[n], a_send.at[n], a_recv.at[n], (me, partner))
            )

        def send(src, dst, n, at, peer):
            return remote(src, dst, b_send.at[n, at], b_recv.at[n, at], (me, peer))

        def chip_sum(n):
            cols = slice(n * cut, (n + 1) * cut)
            a_copy[n].wait_recv()
            for other in range(YN):
                sums[other * 2 + core, :, cols] += a_in[n, other].astype(jnp.float32)
            far_out[n] = sums[op * 2 + core, :, cols].astype(jnp.bfloat16)
            opposite.append(
                (
                    send(far_out.at[n, lo], far_in.at[n, lo], n, 0, y_up),
                    send(far_out.at[n, hi], far_in.at[n, hi], n, 1, y_dn),
                )
            )
            near_out[n, 0, half:, :] = sums[up * 2 + core, half:, cols].astype(jnp.bfloat16)
            near_out[n, 1, :half, :] = sums[dn * 2 + core, :half, cols].astype(jnp.bfloat16)
            lone.append(
                (
                    send(near_out.at[n, 0, hi], near_in.at[n, 0, hi], n, 2, y_up),
                    send(near_out.at[n, 1, lo], near_in.at[n, 1, lo], n, 3, y_dn),
                )
            )

        def pass_on(n):
            cols = slice(n * cut, (n + 1) * cut)
            for copy in opposite[n]:
                copy.wait_recv()
            mine = sums[up * 2 + core, :half, cols] + far_in[n, :half, :].astype(jnp.float32)
            near_out[n, 0, :half, :] = mine.astype(jnp.bfloat16)
            mine = sums[dn * 2 + core, half:, cols] + far_in[n, half:, :].astype(jnp.float32)
            near_out[n, 1, half:, :] = mine.astype(jnp.bfloat16)
            shared.append(
                (
                    send(near_out.at[n, 0, lo], near_in.at[n, 0, lo], n, 4, y_up),
                    send(near_out.at[n, 1, hi], near_in.at[n, 1, hi], n, 5, y_dn),
                )
            )

        def stream(n):
            cols = slice(n * cut, (n + 1) * cut)
            for copy in lone[n] + shared[n]:
                copy.wait_recv()
            branch = sums[tens, :, cols]
            for side in range(2):
                branch += near_in[n, side].astype(jnp.float32)
            keep = drop_ref[:, cols].astype(jnp.float32) * (1.0 / keep_rate)
            value = residual_ref[:, cols].astype(jnp.float32) + keep * branch
            sums[tens, :, cols] = value
            next_ref[:, cols] = value.astype(jnp.bfloat16)
            return jnp.sum(value, axis=1, keepdims=True)

        tally = jnp.zeros((own, 1), jnp.float32)
        for n in range(CUTS + 2):
            if n < CUTS:
                chip_sum(n)
            if 1 <= n <= CUTS:
                pass_on(n - 1)
            if n >= 2:
                tally += stream(n - 2)
        centre = tally / width
        spread = jnp.zeros((own, 1), jnp.float32)
        for at in range(0, width, cut):
            off = sums[tens, :, at : at + cut] - centre
            spread += jnp.sum(off * off, axis=1, keepdims=True)
        scale = lax.rsqrt(spread / width + norm_eps)
        for at in range(0, width, cut):
            cols = slice(at, at + cut)
            normed = (sums[tens, :, cols] - centre) * scale * gain_ref[:, cols] + bias_ref[:, cols]
            normed_ref[:, cols] = normed.astype(jnp.bfloat16)

    halo = []
    live = {"c": gather_codes(), "w": gather_weight()}
    parts = {"g": gather, "k": stores, "r": reduce}
    for step in ORDER:
        for name in step:
            if name not in live:
                live[name] = parts[name[0]](int(name[1:]))
            next(live[name], None)
    for it in live.values():
        for _ in it:
            pass
    project()
    for copy in started + list(pending.values()):
        copy.wait_send()


def layer(owner, slot, q, k, v, weight, residual, drop, gain, bias):
    total, depth = q.shape
    blocks = owner.shape[0]
    groups = depth // (GROUP * HEAD)
    span = total // blocks
    deep, wide = HEAD, GROUP * span
    rows = k.shape[0]
    zn = lax.axis_size("dp") // XN
    steps = zn // 2
    bf, f32 = jnp.bfloat16, jnp.float32
    own, width = residual.shape
    cut = width // CUTS
    per_group = [
        pltpu.VMEM((zn * blocks, deep, wide), bf),
        pltpu.VMEM((XN, rows, k.shape[1], GROUP * HEAD), bf),
        pltpu.VMEM((XN, rows, GROUP * HEAD, v.shape[1]), bf),
        pltpu.VMEM((zn * XN, deep, wide), bf),
        pltpu.VMEM((zn, 8, wide), f32),
        pltpu.VMEM((4, steps + 1, blocks // 2, deep, wide), bf),
        pltpu.VMEM((2, steps + 1, 8, wide), f32),
    ]
    dma = pltpu.SemaphoreType.DMA
    vmem = pl.BlockSpec(memory_space=pltpu.VMEM)
    hbm = pl.BlockSpec(memory_space=pl.ANY)
    ring = dma((groups, 4, steps))
    two = dma((groups, 4, 2))
    return pl.pallas_call(
        functools.partial(layer_kernel, zn, blocks),
        out_shape=[jax.ShapeDtypeStruct(residual.shape, bf)] * 2,
        in_specs=[vmem] * 3 + [hbm, hbm, vmem, hbm, hbm, vmem, vmem],
        out_specs=[vmem, vmem],
        scratch_shapes=per_group * groups
        + [
            pltpu.VMEM((zn, 8, HEAD), jnp.int32),
            pltpu.SMEM((zn, 8, HEAD), jnp.int32),
            pltpu.SMEM((zn, 2 * XN + 2 * blocks), jnp.int32),
            dma((2, 2)),
            dma((2, steps)),
            two,
            ring,
            dma((groups,)),
            dma((groups, 2, 6)),
            dma((groups, 2, 6)),
            two,
            ring,
            dma((groups, 2, 2)),
            dma((groups, 2, steps)),
            dma,
            pltpu.VMEM((zn, XN) + weight.shape, bf),
            pltpu.VMEM((4 * groups, 8, wide), f32),
            pltpu.VMEM((blocks * span + 8, depth), f32),
            pltpu.VMEM((2 * YN, own, width), f32),
            pltpu.VMEM((CUTS, YN, own, cut), bf),
            pltpu.VMEM((CUTS, YN, own, cut), bf),
            pltpu.VMEM((CUTS, own, cut), bf),
            pltpu.VMEM((CUTS, own, cut), bf),
            pltpu.VMEM((CUTS, 2, own, cut), bf),
            pltpu.VMEM((CUTS, 2, own, cut), bf),
            dma((2, 2)),
            dma((2, steps)),
            dma((6,)),
            dma((6,)),
            dma((groups,)),
            dma((groups,)),
            dma((CUTS,)),
            dma((CUTS,)),
            dma((CUTS, 6)),
            dma((CUTS, 6)),
            pltpu.VMEM((8 + total, depth), f32),
            pltpu.VMEM((groups, rows, v.shape[1], GROUP * HEAD), bf),
            dma,
            dma,
            dma((groups,)),
            pltpu.VMEM(residual.shape, residual.dtype),
            pltpu.VMEM(drop.shape, drop.dtype),
            dma((2,)),
        ],
        compiler_params=pltpu.CompilerParams(
            collective_id=0, has_side_effects=True, vmem_limit_bytes=56 * 1024 * 1024
        ),
        cost_estimate=pl.CostEstimate(
            flops=2_200_000_000, bytes_accessed=6_000_000, transcendentals=2_200_000
        ),
    )(owner, slot, q, k, v, weight, residual, drop, gain, bias)


def local(
    queries,
    neighbour_keys,
    neighbour_values,
    residual,
    out_weight,
    drop_mask,
    norm_gain,
    norm_bias,
    neighbour_owner,
    neighbour_slot,
):
    return tuple(
        layer(
            neighbour_owner,
            neighbour_slot,
            queries,
            neighbour_keys,
            neighbour_values,
            out_weight.T,
            residual,
            drop_mask,
            norm_gain.reshape(1, -1),
            norm_bias.reshape(1, -1),
        )
    )


def solution(mesh):
    placed = (
        P("dp", "tensor"),
        P("dp", None, "tensor"),
        P("dp", None, "tensor"),
        P(("dp", "tensor"), None),
        P("tensor", "dp"),
        P(("dp", "tensor"), None),
        P(),
        P(),
        P("dp", None),
        P("dp", None),
    )
    return jax.shard_map(
        local,
        mesh=mesh,
        in_specs=placed,
        out_specs=(P(("dp", "tensor"), None), P(("dp", "tensor"), None)),
        check_vma=False,
    )
```
